128 devices in a mesh: slide: 32 (over y, x, core), row: 4 (over z).
Axes of the slice: x: 4, y: 4, z: 4, core: 2. Of those that a mesh axis runs over, the one named last changes fastest.
Arguments:
- tiles: bfloat16 [32, 4, 64, 16, 768], P('slide', None, 'row'), may hold values from -6 to 6
- cotangent: bfloat16 [32, 4, 64, 16, 768], P('slide', None, 'row'), may hold values from -6 to 6
- tile_counts: int32 [32], P('slide'), may hold values from 1 to 3, as said below
- dw_kernel: float32 [7, 7, 768], replicated, may hold values from -0.875 to 0.875
- ln_gain: float32 [768], replicated, may hold values from 0.5 to 1.5
- fc1_weight: bfloat16 [3072, 768], replicated, may hold values from -0.21875 to 0.21875
- fc2_weight: bfloat16 [768, 3072], replicated, may hold values from -0.109375 to 0.109375
- layer_scale: float32 [768], replicated, may hold values from 0.3 to 1.5
Outputs:
- block_out: bfloat16 [32, 4, 64, 16, 768], P('slide', None, 'row')
- grad_input: float32 [32, 4, 64, 16, 768], P('slide', None, 'row')
- grad_fc1: float32 [3072, 768], P(('slide', 'row'))
- grad_fc2: float32 [768, 3072], P(('slide', 'row'))
- grad_kernel: float32 [7, 7, 768], replicated
- grad_gain: float32 [768], replicated
- grad_scale: float32 [768], replicated
The draws below stay inside these ranges and needn't reach their ends.
Inputs may be any that keep to these rules, and one draw needn't show every extreme that they name: For s < 16, tile_counts[s] + tile_counts[s + 16] = 4.
All inputs are finite; a program needn't handle non-finite values.
Results may differ from the reference program's by a relative error of at most 0.0062.
Values may be sent and summed in bfloat16 or wider, within the bound.
No kernel may reach another device: no remote copies, remote signals or barrier semaphores. Data moves between devices by JAX's collectives and lax.ppermute only.
A program may use at most 192 MiB of HBM per device.

```python
import math
import jax
import jax.numpy as jnp
from jax import lax

C = 768
FF = 3072
SLOTS = 4
WT = 16
TILE_H = 64
N_SLIDE = 32


def draw_tile_counts(key, part):
    key = jax.random.fold_in(key, 7)
    first_half = jax.random.randint(key, (N_SLIDE // 2,), 1, SLOTS)
    first_half = first_half.at[0].set(SLOTS - 1)
    return jnp.concatenate([first_half, SLOTS - first_half]).astype(jnp.int32)


def levels(stream_key, shape, shards, smallest, largest):
    loudness, own = 1.0, jax.random.fold_in(stream_key, 6)
    for position, shards_of in shards:
        heights = jnp.exp(jax.random.uniform(jax.random.fold_in(own, position), (shards_of,), jnp.float32, smallest / len(shards), largest / len(shards)))
        loudness = loudness * jnp.repeat(heights, shape[position] // shards_of).reshape([-1 if axis == position else 1 for axis in range(len(shape))])
    return loudness


def bell_draw(own_key, dims, scale, reach, shards=(), kind=jnp.bfloat16):
    drawn = scale * jax.random.normal(own_key, dims, jnp.float32)
    if shards:
        drawn = drawn * levels(own_key, dims, shards, -0.22, 0.18)
    return jnp.clip(drawn, -reach, reach).astype(kind)


def setup_inputs(seed: int = 0) -> dict:
    key_of = jax.random.split(jax.random.key(seed), 9)
    return {
        "tiles": bell_draw(key_of[0], (N_SLIDE, SLOTS, TILE_H, WT, C), 1.0, 6.0, ((0, 32), (2, 4))),
        "cotangent": bell_draw(key_of[1], (N_SLIDE, SLOTS, TILE_H, WT, C), 1.0, 6.0, ((0, 32), (2, 4))),
        "tile_counts": draw_tile_counts(jax.random.fold_in(key_of[8], 71), 0),
        "dw_kernel": bell_draw(key_of[3], (7, 7, C), 49 ** -0.5, 0.875, (), jnp.float32),
        "ln_gain": jnp.clip(1.0 + 0.1 * jax.random.normal(key_of[4], (C,), jnp.float32), 0.5, 1.5),
        "fc1_weight": bell_draw(key_of[5], (FF, C), C ** -0.5, 0.21875),
        "fc2_weight": bell_draw(key_of[6], (C, FF), FF ** -0.5, 0.109375),
        "layer_scale": jnp.clip(jnp.exp(jax.random.uniform(key_of[7], (C,), jnp.float32, math.log(0.3), math.log(1.5))), 0.3, 1.5),
    }


epsilon = 1e-06
root_half = 1.0 / math.sqrt(2.0)
density = 1.0 / math.sqrt(2.0 * math.pi)

def gelu_exact(values):
    return 0.5 * values * (1.0 + jax.scipy.special.erf(values * root_half))

def gelu_slope(values):
    return 0.5 * (1.0 + jax.scipy.special.erf(values * root_half)) + values * jnp.exp(-0.5 * values * values) * density

def tile_pass(tile_in, cotan, kernel, gain, first, second, scale):
    height, width, chans = tile_in.shape
    padded = jnp.pad(tile_in.astype(jnp.float32), ((3, 3), (3, 3), (0, 0)))
    filtered = jnp.zeros((height, width, chans), jnp.float32)
    for tap_row in range(7):
        for tap_col in range(7):
            filtered = filtered + kernel[tap_row, tap_col] * padded[tap_row:tap_row + height, tap_col:tap_col + width]
    center = filtered - lax.optimization_barrier(jnp.mean(filtered, axis=-1, keepdims=True))
    inv_std = lax.rsqrt(lax.optimization_barrier(jnp.mean(center * center, axis=-1, keepdims=True)) + epsilon)
    unit = center * inv_std
    normed = (unit * gain).astype(jnp.bfloat16).reshape(-1, chans)
    pre = jnp.dot(normed, first.T, preferred_element_type=jnp.float32)
    act = gelu_exact(pre).astype(jnp.bfloat16)
    branch = jnp.dot(act, second.T, preferred_element_type=jnp.float32).reshape(height, width, chans)
    out = (tile_in.astype(jnp.float32) + scale * branch).astype(jnp.bfloat16)
    held = cotan.astype(jnp.float32)
    scale_grad = lax.optimization_barrier(jnp.sum(held * branch, axis=(0, 1)))
    d_branch = (scale * held).astype(jnp.bfloat16).reshape(-1, chans)
    second_grad = jnp.dot(d_branch.T, act, preferred_element_type=jnp.float32)
    d_act = jnp.dot(d_branch, second, preferred_element_type=jnp.float32)
    d_pre = (d_act * gelu_slope(pre)).astype(jnp.bfloat16)
    first_grad = jnp.dot(d_pre.T, normed, preferred_element_type=jnp.float32)
    d_normed = jnp.dot(d_pre, first, preferred_element_type=jnp.float32).reshape(height, width, chans)
    gain_grad = lax.optimization_barrier(jnp.sum(d_normed * unit, axis=(0, 1)))
    scaled = d_normed * gain
    d_filt = inv_std * (scaled - lax.optimization_barrier(jnp.mean(scaled, axis=-1, keepdims=True)) - unit * lax.optimization_barrier(jnp.mean(scaled * unit, axis=-1, keepdims=True)))
    kernel_grad = jnp.stack([jnp.stack([lax.optimization_barrier(jnp.sum(padded[tap_row:tap_row + height, tap_col:tap_col + width] * d_filt, axis=(0, 1))) for tap_col in range(7)]) for tap_row in range(7)])
    beside_all = jnp.pad(d_filt, ((3, 3), (3, 3), (0, 0)))
    input_grad = held
    for tap_row in range(7):
        for tap_col in range(7):
            input_grad = input_grad + kernel[tap_row, tap_col] * beside_all[6 - tap_row:6 - tap_row + height, 6 - tap_col:6 - tap_col + width]
    return (out, input_grad, first_grad, second_grad, kernel_grad, gain_grad, scale_grad)

def reference(tiles, cotangent, tile_counts, dw_kernel, ln_gain, fc1_weight, fc2_weight, layer_scale):
    slides, slots, height, width, chans = tiles.shape
    flat_tiles = tiles.reshape(slides * slots, height, width, chans)
    flat_cotan = cotangent.reshape(slides * slots, height, width, chans)
    live = (jnp.arange(slots, dtype=jnp.int32)[None, :] < tile_counts[:, None]).reshape(-1)
    hidden = fc1_weight.shape[0]

    def dead_pass(tile_in, cotan):
        return (jnp.zeros((height, width, chans), jnp.bfloat16), jnp.zeros((height, width, chans), jnp.float32), jnp.zeros((hidden, chans), jnp.float32), jnp.zeros((chans, hidden), jnp.float32), jnp.zeros((7, 7, chans), jnp.float32), jnp.zeros((chans,), jnp.float32), jnp.zeros((chans,), jnp.float32))

    def live_pass(tile_in, cotan):
        return tile_pass(tile_in, cotan, dw_kernel, ln_gain, fc1_weight, fc2_weight, layer_scale)

    def step(carry, item):
        tile_in, cotan, alive = item
        result = lax.cond(alive, live_pass, dead_pass, tile_in, cotan)
        carry = tuple((total + term for total, term in zip(carry, result[2:])))
        return (carry, (result[0], result[1]))
    start = (jnp.zeros((hidden, chans), jnp.float32), jnp.zeros((chans, hidden), jnp.float32), jnp.zeros((7, 7, chans), jnp.float32), jnp.zeros((chans,), jnp.float32), jnp.zeros((chans,), jnp.float32))
    sums, (outs, grads) = lax.scan(step, start, (flat_tiles, flat_cotan, live))
    block_out = outs.reshape(slides, slots, height, width, chans)
    grad_input = grads.reshape(slides, slots, height, width, chans)
    return (block_out, grad_input, sums[0], sums[1], sums[2], sums[3], sums[4])
```

```python
import math

import jax
import jax.numpy as jnp
from jax import lax
from jax.sharding import PartitionSpec as P

epsilon = 1e-06
root_half = 1.0 / math.sqrt(2.0)
density = 1.0 / math.sqrt(2.0 * math.pi)


def with_halo(cells, sides, width):
    for axis, dim in sides:
        count = lax.axis_size(axis)
        ends = count - 1
        head = lax.slice_in_dim(cells, 0, width, axis=dim)
        tail = lax.slice_in_dim(cells, cells.shape[dim] - width, cells.shape[dim], axis=dim)
        cells = jnp.concatenate(
            [
                lax.ppermute(tail, axis, [(i, (i + 1) % count) for i in range(ends)]),
                cells,
                lax.ppermute(head, axis, [((i + 1) % count, i) for i in range(ends)]),
            ],
            axis=dim,
        )
    return cells


def shifted(value, axis, by):
    peers = lax.axis_size(axis)
    pairs = [(i, i + by) for i in range(peers) if 0 <= i + by < peers]
    return lax.ppermute(value, axis, pairs)


def gelu_exact(values):
    return 0.5 * values * (1.0 + jax.scipy.special.erf(values * root_half))


def gelu_slope(values):
    return (
        0.5 * (1.0 + jax.scipy.special.erf(values * root_half))
        + values * jnp.exp(-0.5 * values * values) * density
    )


def same_core_groups():
    slides, rows = lax.axis_size("slide"), lax.axis_size("row")
    return [[s * rows + r for s in range(c, slides, 2) for r in range(rows)] for c in range(2)]


def reduced_share(term):
    slides, rows = lax.axis_size("slide"), lax.axis_size("row")
    core = lax.axis_index("slide") % 2
    halves = term.astype(jnp.bfloat16).reshape(slides // 2, 2, -1, term.shape[1])
    mine = lax.dynamic_index_in_dim(halves, core, 1, keepdims=False)
    other = lax.dynamic_index_in_dim(halves, 1 - core, 1, keepdims=False)
    got = lax.ppermute(other, "slide", [(i, i ^ 1) for i in range(slides)])
    chip = (mine.astype(jnp.float32) + got.astype(jnp.float32)).astype(jnp.bfloat16)
    chip = chip.reshape(-1, term.shape[1])
    parts = lax.all_to_all(
        chip, ("slide", "row"), 0, 0, axis_index_groups=same_core_groups(), tiled=True
    )
    parts = parts.reshape(slides * rows // 2, -1, term.shape[1])
    return jnp.sum(parts.astype(jnp.float32), axis=0)


def summed_everywhere(values):
    axes = ("slide", "row")
    count = lax.axis_size("slide") * lax.axis_size("row")
    flat = values.reshape(-1)
    lanes = -(-flat.size // (count * 128)) * 128
    padded = jnp.pad(flat, (0, count * lanes - flat.size)).reshape(count, lanes)
    share = jnp.sum(lax.all_to_all(padded, axes, 0, 0, tiled=True), axis=0)
    whole = lax.all_to_all(jnp.broadcast_to(share, (count, lanes)), axes, 0, 0, tiled=True)
    return whole.reshape(-1)[: flat.size].reshape(values.shape)


def block_pass(tiles_in, cotan, alive, kernel, gain, first, second, scale):
    slots, rows, cols, chans = tiles_in.shape
    extended = with_halo(tiles_in, (("row", 1),), 3)
    padded = jnp.pad(extended.astype(jnp.float32), ((0, 0), (0, 0), (3, 3), (0, 0)))
    filtered = jnp.zeros((slots, rows, cols, chans), jnp.float32)
    for tap_row in range(7):
        for tap_col in range(7):
            filtered = (
                filtered
                + kernel[tap_row, tap_col]
                * padded[:, tap_row : tap_row + rows, tap_col : tap_col + cols]
            )
    center = filtered - jnp.mean(filtered, axis=-1, keepdims=True)
    inv_std = lax.rsqrt(jnp.mean(center * center, axis=-1, keepdims=True) + epsilon)
    unit = center * inv_std
    normed = (unit * gain).astype(jnp.bfloat16).reshape(-1, chans)
    pre = lax.dot_general(
        normed, first, (((1,), (1,)), ((), ())), preferred_element_type=jnp.float32
    )
    act = gelu_exact(pre).astype(jnp.bfloat16)
    branch = lax.dot_general(
        act, second, (((1,), (1,)), ((), ())), preferred_element_type=jnp.float32
    )
    branch = branch.reshape(slots, rows, cols, chans)
    weight = alive.astype(jnp.float32)[:, None, None, None]
    out = ((tiles_in.astype(jnp.float32) + scale * branch) * weight).astype(jnp.bfloat16)
    held = cotan.astype(jnp.float32) * weight
    scale_grad = jnp.sum(held * branch, axis=(0, 1, 2))
    d_branch = (scale * held).astype(jnp.bfloat16).reshape(-1, chans)
    second_grad = lax.dot_general(
        d_branch, act, (((0,), (0,)), ((), ())), preferred_element_type=jnp.float32
    )
    d_act = jnp.dot(d_branch, second, preferred_element_type=jnp.float32)
    d_pre = (d_act * gelu_slope(pre)).astype(jnp.bfloat16)
    first_grad = lax.dot_general(
        d_pre, normed, (((0,), (0,)), ((), ())), preferred_element_type=jnp.float32
    )
    d_normed = jnp.dot(d_pre, first, preferred_element_type=jnp.float32).reshape(
        slots, rows, cols, chans
    )
    gain_grad = jnp.sum(d_normed * unit, axis=(0, 1, 2))
    scaled = d_normed * gain
    d_filt = inv_std * (
        scaled
        - jnp.mean(scaled, axis=-1, keepdims=True)
        - unit * jnp.mean(scaled * unit, axis=-1, keepdims=True)
    )
    kernel_grad = jnp.stack(
        [
            jnp.stack(
                [
                    jnp.sum(
                        padded[:, tap_row : tap_row + rows, tap_col : tap_col + cols] * d_filt,
                        axis=(0, 1, 2),
                    )
                    for tap_col in range(7)
                ]
            )
            for tap_row in range(7)
        ]
    )
    local = jnp.pad(d_filt, ((0, 0), (6, 6), (3, 3), (0, 0)))
    spread = jnp.zeros((slots, rows + 6, cols, chans), jnp.float32)
    for tap_row in range(7):
        for tap_col in range(7):
            spread = (
                spread
                + kernel[tap_row, tap_col]
                * local[:, 6 - tap_row : 12 - tap_row + rows, 6 - tap_col : 6 - tap_col + cols]
            )
    from_below = shifted(spread[:, :3].astype(jnp.bfloat16), "row", -1).astype(jnp.float32)
    from_above = shifted(spread[:, rows + 3 :].astype(jnp.bfloat16), "row", 1).astype(jnp.float32)
    back = spread[:, 3 : rows + 3]
    back = back.at[:, :3].add(from_above)
    back = back.at[:, rows - 3 :].add(from_below)
    input_grad = held + back
    return (out, input_grad, first_grad, second_grad, kernel_grad, gain_grad, scale_grad)


def body(tiles, cotangent, tile_counts, dw_kernel, ln_gain, fc1_weight, fc2_weight, layer_scale):
    tiles_in = tiles[0]
    cotan_in = cotangent[0]
    slots = tiles_in.shape[0]
    count = tile_counts[0]
    slot_ids = jnp.arange(slots, dtype=jnp.int32)
    results = block_pass(
        tiles_in,
        cotan_in,
        slot_ids < count,
        dw_kernel,
        ln_gain,
        fc1_weight,
        fc2_weight,
        layer_scale,
    )
    block_out = results[0]
    grad_input = results[1]
    first_term = results[2]
    second_term = results[3]
    grad_fc1 = reduced_share(first_term)
    grad_fc2 = reduced_share(second_term.reshape(first_term.shape)).reshape(-1, second_term.shape[1])
    small = jnp.concatenate([results[4].reshape(49, -1), results[5][None], results[6][None]])
    small = summed_everywhere(small)
    grad_kernel, grad_gain, grad_scale = small[:49].reshape(7, 7, -1), small[49], small[50]
    return (
        block_out[None],
        grad_input[None],
        grad_fc1,
        grad_fc2,
        grad_kernel,
        grad_gain,
        grad_scale,
    )


def solution(mesh):
    in_specs = (
        P("slide", None, "row", None, None),
        P("slide", None, "row", None, None),
        P("slide"),
        P(),
        P(),
        P(),
        P(),
        P(),
    )
    out_specs = (
        P("slide", None, "row", None, None),
        P("slide", None, "row", None, None),
        P(("slide", "row"), None),
        P(("slide", "row"), None),
        P(),
        P(),
        P(),
    )
    return jax.shard_map(body, mesh=mesh, in_specs=in_specs, out_specs=out_specs, check_vma=False)
```

```python
import functools
import math

import jax
import jax.numpy as jnp
from jax import lax
from jax.experimental import pallas as pl
from jax.experimental.pallas import tpu as pltpu
from jax.sharding import PartitionSpec as P

epsilon = 1e-06
root_half = 1.0 / math.sqrt(2.0)
density = 1.0 / math.sqrt(2.0 * math.pi)
f32, bf16 = jnp.float32, jnp.bfloat16
REACH = 3
TAPS = 7
LEFT = 8
LANES = 128
MOST = 3
BLOCK = 768
CUT = 256


def same_core_groups():
    slides, rows = lax.axis_size("slide"), lax.axis_size("row")
    return [[s * rows + r for s in range(c, slides, 2) for r in range(rows)] for c in range(2)]


def after(*values):
    return lax.optimization_barrier(values)


def core_halves(term):
    slides = lax.axis_size("slide")
    core = lax.axis_index("slide") % 2
    halves = term.reshape(slides // 2, 2, -1, term.shape[1])
    mine = lax.dynamic_index_in_dim(halves, core, 1, keepdims=False)
    other = lax.dynamic_index_in_dim(halves, 1 - core, 1, keepdims=False)
    return mine, other


def from_other_core(half):
    return lax.ppermute(half, "slide", [(i, i ^ 1) for i in range(lax.axis_size("slide"))])


def exchanged(chip):
    return lax.all_to_all(
        chip.reshape(-1, chip.shape[-1]),
        ("slide", "row"),
        0,
        0,
        axis_index_groups=same_core_groups(),
        tiled=True,
    )


def added(parts):
    peers = lax.axis_size("slide") * lax.axis_size("row") // 2
    return jnp.sum(parts.reshape(peers, -1, parts.shape[-1]).astype(f32), axis=0)


def lane_major(chip):
    peers = lax.axis_size("slide") * lax.axis_size("row") // 2
    cells = chip.reshape(peers, -1, chip.shape[-1] // LANES, LANES)
    return jnp.swapaxes(cells, 1, 2).reshape(peers, -1, LANES)


def with_small(chip, small):
    cells = lane_major(chip)
    peers = cells.shape[0]
    share = -(-small.size // (peers * 8 * LANES)) * 8
    flat = jnp.pad(small.reshape(-1), (0, peers * share * LANES - small.size))
    return jnp.concatenate([cells, flat.astype(bf16).reshape(peers, share, LANES)], axis=1)


def everywhere(share, like):
    slides, rows = lax.axis_size("slide"), lax.axis_size("row")
    sent = jnp.broadcast_to(share[None], (slides * rows, *share.shape))
    got = lax.all_to_all(sent, ("slide", "row"), 0, 0, tiled=True)
    got = jnp.sum(got.reshape(slides // 2, 2, rows, -1), axis=1)
    return got.reshape(-1)[: like.size].reshape(like.shape)


def edges(cells):
    ends = lax.axis_size("row") - 1
    head = cells[:, :REACH]
    tail = cells[:, cells.shape[1] - REACH :]
    above = lax.ppermute(tail, "row", [(i, i + 1) for i in range(ends)])
    below = lax.ppermute(head, "row", [(i + 1, i) for i in range(ends)])
    return above, below


def fill_padded(pad, above_ref, cells_ref, below_ref, rows, cols):
    zeros = jnp.zeros((rows + 2 * REACH, LEFT, pad.shape[2]), f32)
    pad[:, 0:LEFT, :] = zeros
    pad[:, LEFT + cols : 2 * LEFT + cols, :] = zeros
    inner = pl.ds(LEFT, cols)
    pad[0:REACH, inner, :] = above_ref[0].astype(f32)
    pad[REACH : REACH + rows, inner, :] = cells_ref[...].reshape(rows, cols, -1).astype(f32)
    pad[REACH + rows : rows + 2 * REACH, inner, :] = below_ref[0].astype(f32)


def lane_blocks(chans, body):
    def step(i, carry):
        body(pl.ds(pl.multiple_of(i * LANES, LANES), LANES))
        return carry

    lax.fori_loop(0, chans // LANES, step, 0)


def stencil(pad, wide, rows, cols, flip, emit):
    def over(lanes):
        for half in range(cols // 8):
            total = [jnp.zeros((8, LANES), f32) for _ in range(rows)]
            for b in range(TAPS):
                at = pl.ds(LEFT - REACH + b + 8 * half, 8)
                line = [pad[r, at, lanes] for r in range(rows + 2 * REACH)]
                for a in range(TAPS):
                    tap = a * TAPS + b
                    weight = wide[TAPS * TAPS - 1 - tap if flip else tap, :, lanes]
                    for p in range(rows):
                        total[p] = total[p] + weight * line[p + a]
            for p in range(rows):
                emit(p, half, lanes, total[p])

    lane_blocks(pad.shape[2], over)


def spread_kernel(wide, kernel_ref):
    for tap in range(TAPS * TAPS):
        wide[tap] = jnp.broadcast_to(kernel_ref[tap : tap + 1, :], wide.shape[1:])


def forward_kernel(
    count, tiles, above, below, cotan, kernel, gain, scale, normed, unit, spread, held_out, pad, wide, filt
):
    slot = pl.program_id(0)
    rows, cols, chans = tiles.shape[2:]

    @pl.when(slot == 0)
    def _():
        spread_kernel(wide, kernel)

    fill_padded(pad, above, tiles, below, rows, cols)

    def emit(p, half, lanes, value):
        filt[pl.ds(p * cols + 8 * half, 8), lanes] = value

    stencil(pad, wide, rows, cols, False, emit)
    weight = (slot < count[0]).astype(f32)
    held = cotan[...].reshape(rows * cols, chans).astype(f32) * weight
    held_out[...] = (held * scale[...]).astype(bf16)

    def norm(i, carry):
        at = pl.ds(pl.multiple_of(i * 32, 32), 32)
        value = filt[at, :]
        center = value - jnp.mean(value, axis=-1, keepdims=True)
        inv_std = lax.rsqrt(jnp.mean(center * center, axis=-1, keepdims=True) + epsilon)
        one = center * inv_std
        unit[at, :] = one
        normed[at, :] = (one * gain[...]).astype(bf16)
        spread[at, :] = jnp.broadcast_to(inv_std, (32, LANES))
        return carry

    lax.fori_loop(0, rows * cols // 32, norm, 0)


def gelu_parts(pre):
    size = jnp.abs(pre)
    bell = jnp.exp(pre * pre * -0.5)
    t = 1.0 / (1.0 + (0.3275911 * root_half) * size)
    poly = t * (
        0.5 * 0.254829592
        + t * (0.5 * -0.284496736 + t * (0.5 * 1.421413741 + t * (0.5 * -1.453152027 + t * (0.5 * 1.061405429))))
    )
    tail = poly * bell
    return jnp.where(pre < 0.0, tail, 1.0 - tail), bell * density


def hidden_kernel(normed, spread, first, act, slope, term, turned, total):
    step = pl.program_id(0)

    @pl.when(step == 0)
    def _():
        turned[...] = spread[...].T

    for part in range(BLOCK // CUT):
        cut = slice(part * CUT, (part + 1) * CUT)
        pre = lax.dot_general(
            normed[...], first[cut, :], (((1,), (1,)), ((), ())), preferred_element_type=f32
        )
        cdf, pdf = gelu_parts(pre)
        active = (pre * cdf).astype(bf16)
        act[:, cut] = active
        slope[:, cut] = (cdf + pre * pdf).astype(bf16)
        grad = jnp.dot(turned[...], active, preferred_element_type=f32)
        for lane in range(CUT // LANES):
            total[part * (CUT // LANES) + lane, pl.ds(step, grad.shape[0], stride=4), :] = grad[
                :, lane * LANES : (lane + 1) * LANES
            ]

    @pl.when(step == pl.num_programs(0) - 1)
    def _():
        for lane in range(BLOCK // LANES):
            term[:, lane * LANES : (lane + 1) * LANES] = total[lane].astype(bf16)


def back_kernel(
    normed, spread, slope, first, second, unit, inv, gain, term, d_filt, gain_grad, total, d_pre
):
    step = pl.program_id(0)
    pixels, chans = normed.shape
    for part in range(BLOCK // CUT):
        cut = slice(part * CUT, (part + 1) * CUT)
        d_act = jnp.dot(spread[...], second[:, cut], preferred_element_type=f32)
        d_cut = (d_act * slope[:, cut].astype(f32)).astype(bf16)
        d_pre[:, cut] = d_cut
        term[cut, :] = lax.dot_general(
            d_cut, normed[...], (((0,), (0,)), ((), ())), preferred_element_type=f32
        ).astype(bf16)
    d_normed = jnp.dot(d_pre[...], first[...], preferred_element_type=f32)

    @pl.when(step == 0)
    def _():
        total[...] = d_normed

    @pl.when(step > 0)
    def _():
        total[...] += d_normed

    @pl.when(step == pl.num_programs(0) - 1)
    def _():
        def norm(i, kept):
            at = pl.ds(pl.multiple_of(i * 16, 16), 16)
            grad, one = total[at, :], unit[at, :]
            turn = grad * one
            kept = kept + (turn[:8] + turn[8:])
            scaled = grad * gain[...]
            mean = jnp.mean(scaled, axis=-1, keepdims=True)
            along = jnp.mean(scaled * one, axis=-1, keepdims=True)
            d_filt[at, :] = inv[at, 0:1] * (scaled - mean - one * along)
            return kept

        gain_grad[...] = lax.fori_loop(0, pixels // 16, norm, jnp.zeros((8, chans), f32))


def tap_kernel(tiles, above, below, d_filt, grad, pad, total):
    slot = pl.program_id(0)
    rows, cols, chans = tiles.shape[2:]
    fill_padded(pad, above, tiles, below, rows, cols)

    @pl.when(slot == 0)
    def _():
        total[...] = jnp.zeros_like(total)

    def over(lanes):
        for half in range(cols // 8):
            back = [d_filt[pl.ds(p * cols + 8 * half, 8), lanes] for p in range(rows)]
            for b in range(TAPS):
                at = pl.ds(LEFT - REACH + b + 8 * half, 8)
                line = [pad[r, at, lanes] for r in range(rows + 2 * REACH)]
                for a in range(TAPS):
                    acc = line[a] * back[0]
                    for p in range(1, rows):
                        acc = acc + line[p + a] * back[p]
                    total[a * TAPS + b, :, lanes] += acc

    lane_blocks(chans, over)

    @pl.when(slot == pl.num_programs(0) - 1)
    def _():
        for tap in range(TAPS * TAPS):
            grad[tap : tap + 1, :] = jnp.sum(total[tap], axis=0, keepdims=True)


def input_kernel(count, d_filt, above, below, cotan, kernel, out, pad, wide):
    slot = pl.program_id(0)
    rows, cols, chans = out.shape[2:]

    @pl.when(slot == 0)
    def _():
        spread_kernel(wide, kernel)

    @pl.when(slot < MOST)
    def _():
        fill_padded(pad, above, d_filt, below, rows, cols)
        weight = (slot < count[0]).astype(f32)

        def emit(p, half, lanes, value):
            at = pl.ds(8 * half, 8)
            out[0, 0, p, at, lanes] = value + cotan[0, 0, p, at, lanes].astype(f32) * weight

        stencil(pad, wide, rows, cols, True, emit)

    @pl.when(slot >= MOST)
    def _():
        out[...] = jnp.zeros_like(out)


def out_kernel(count, act, second, tiles, cotan, scale, out, scale_grad):
    slot = pl.program_id(0)
    rows, cols, chans = tiles.shape[2:]

    @pl.when(slot == 0)
    def _():
        scale_grad[...] = jnp.zeros_like(scale_grad)

    @pl.when(slot < count[0])
    def _():
        branch = lax.dot_general(
            act[...], second[...], (((1,), (1,)), ((), ())), preferred_element_type=f32
        )
        cells = tiles[...].reshape(rows * cols, chans).astype(f32)
        held = cotan[...].reshape(rows * cols, chans).astype(f32)
        scale_grad[...] += jnp.sum((held * branch).reshape(-1, 8, chans), axis=0)
        out[...] = (cells + scale[...] * branch).astype(bf16).reshape(out.shape)

    @pl.when(slot >= count[0])
    def _():
        out[...] = jnp.zeros_like(out)


def body(tiles, cotangent, tile_counts, dw_kernel, ln_gain, fc1_weight, fc2_weight, layer_scale):
    _, slots, rows, cols, chans = tiles.shape
    hidden = fc1_weight.shape[0]
    pixels = rows * cols
    every = MOST * pixels
    taps = dw_kernel.reshape(TAPS * TAPS, chans)
    gain, scale = ln_gain[None], layer_scale[None]
    above, below = edges(tiles[0, :MOST])

    params = pltpu.CompilerParams(
        vmem_limit_bytes=60 * 1024 * 1024, dimension_semantics=("arbitrary",)
    )
    shape = jax.ShapeDtypeStruct
    brief = pl.CostEstimate(flops=1, bytes_accessed=1, transcendentals=0)
    smem = pl.BlockSpec(memory_space=pltpu.SMEM)
    tile = pl.BlockSpec((1, 1, rows, cols, chans), lambda s: (0, s, 0, 0, 0))
    tile_live = pl.BlockSpec(
        (1, 1, rows, cols, chans), lambda s: (0, jnp.minimum(s, MOST - 1), 0, 0, 0)
    )
    edge = pl.BlockSpec((1, REACH, cols, chans), lambda s: (s, 0, 0, 0))
    edge_live = pl.BlockSpec(
        (1, REACH, cols, chans), lambda s: (jnp.minimum(s, MOST - 1), 0, 0, 0)
    )
    flat = pl.BlockSpec((pixels, chans), lambda s: (s, 0))
    flat_live = pl.BlockSpec((pixels, chans), lambda s: (jnp.minimum(s, MOST - 1), 0))

    def whole(*dims):
        return pl.BlockSpec(dims, lambda s: (0,) * len(dims))

    pad = pltpu.VMEM((rows + 2 * REACH, cols + 2 * LEFT, chans), f32)
    wide = pltpu.VMEM((TAPS * TAPS, 8, chans), f32)

    normed, unit, inv, spread = pl.pallas_call(
        forward_kernel,
        grid=(MOST,),
        in_specs=[smem, tile, edge, edge, tile, whole(TAPS * TAPS, chans), whole(1, chans), whole(1, chans)],
        out_specs=[flat, flat, pl.BlockSpec((pixels, LANES), lambda s: (s, 0)), flat],
        out_shape=[
            shape((every, chans), bf16),
            shape((every, chans), f32),
            shape((every, LANES), f32),
            shape((every, chans), bf16),
        ],
        scratch_shapes=[pad, wide, pltpu.VMEM((pixels, chans), f32)],
        compiler_params=params,
        cost_estimate=brief,
        name="forward",
    )(tile_counts, tiles, above, below, cotangent, taps, gain, scale)

    rows_of = pl.BlockSpec((BLOCK, chans), lambda j: (j, 0))
    cols_of = pl.BlockSpec((chans, BLOCK), lambda j: (0, j))
    wide_of = pl.BlockSpec((every, BLOCK), lambda j: (0, j))
    act, slope, term2 = pl.pallas_call(
        hidden_kernel,
        grid=(hidden // BLOCK,),
        in_specs=[whole(every, chans), whole(every, chans), rows_of],
        out_specs=[wide_of, wide_of, whole(hidden, chans)],
        out_shape=[
            shape((every, hidden), bf16),
            shape((every, hidden), bf16),
            shape((hidden, chans), bf16),
        ],
        scratch_shapes=[pltpu.VMEM((chans, every), bf16), pltpu.VMEM((chans // LANES, hidden, LANES), f32)],
        compiler_params=params,
        cost_estimate=brief,
        name="hidden",
    )(normed, spread, fc1_weight)

    mine2, other2 = core_halves(term2)
    act, other2 = after(act, other2)
    got2 = from_other_core(other2)
    block_out, scale_grad = pl.pallas_call(
        out_kernel,
        grid=(slots,),
        in_specs=[
            smem,
            pl.BlockSpec((pixels, hidden), lambda s: (jnp.minimum(s, MOST - 1), 0)),
            whole(chans, hidden),
            tile_live,
            tile_live,
            whole(1, chans),
        ],
        out_specs=[tile, whole(8, chans)],
        out_shape=[shape(tiles.shape, bf16), shape((8, chans), f32)],
        compiler_params=params,
        cost_estimate=brief,
        name="outs",
    )(tile_counts, act, fc2_weight, tiles, cotangent, scale)

    chip2 = mine2.astype(f32) + got2.astype(f32)
    chip2 = chip2.astype(bf16)
    chip2, slope, block_out = after(chip2, slope, block_out)
    parts2 = exchanged(chip2)

    term1, d_filt, gain_grad = pl.pallas_call(
        back_kernel,
        grid=(hidden // BLOCK,),
        in_specs=[
            whole(every, chans),
            whole(every, chans),
            wide_of,
            rows_of,
            cols_of,
            whole(every, chans),
            whole(every, LANES),
            whole(1, chans),
        ],
        out_specs=[rows_of, whole(every, chans), whole(8, chans)],
        out_shape=[
            shape((hidden, chans), bf16),
            shape((every, chans), f32),
            shape((8, chans), f32),
        ],
        scratch_shapes=[pltpu.VMEM((every, chans), f32), pltpu.VMEM((every, BLOCK), bf16)],
        compiler_params=params,
        cost_estimate=brief,
        name="back",
    )(normed, spread, slope, fc1_weight, fc2_weight, unit, inv, gain)

    mine1, other1 = core_halves(term1)
    d_filt, other1 = after(d_filt, other1)
    got1 = from_other_core(other1)
    d_cells = d_filt.reshape(MOST, rows, cols, chans)
    d_above, d_below = edges(d_cells.astype(bf16))

    tap_grad = pl.pallas_call(
        tap_kernel,
        grid=(MOST,),
        in_specs=[tile, edge, edge, flat],
        out_specs=whole(TAPS * TAPS, chans),
        out_shape=shape((TAPS * TAPS, chans), f32),
        scratch_shapes=[pad, wide],
        compiler_params=params,
        cost_estimate=brief,
        name="taps",
    )(tiles, above, below, d_filt)

    scale_row = jnp.sum(scale_grad, axis=0)
    gain_row = jnp.sum(gain_grad, axis=0)
    small = jnp.concatenate([tap_grad, gain_row[None], scale_row[None]])
    chip1 = with_small(mine1.astype(f32) + got1.astype(f32), small).astype(bf16)
    chip1, parts2 = after(chip1, parts2)
    parts1 = exchanged(chip1)
    d_filt, chip1 = after(d_filt, chip1)

    grad_input = pl.pallas_call(
        input_kernel,
        grid=(slots,),
        in_specs=[smem, flat_live, edge_live, edge_live, tile_live, whole(TAPS * TAPS, chans)],
        out_specs=tile,
        out_shape=shape(tiles.shape, f32),
        scratch_shapes=[pad, wide],
        compiler_params=params,
        cost_estimate=brief,
        name="inputs",
    )(tile_counts, d_filt, d_above, d_below, cotangent, taps)

    grad_fc2 = added(parts2).reshape(-1, hidden)
    sums = added(parts1)
    own = hidden * chans // (LANES * lax.axis_size("slide") * lax.axis_size("row"))
    grad_fc1 = jnp.swapaxes(sums[:own].reshape(chans // LANES, -1, LANES), 0, 1)
    grad_fc1 = grad_fc1.reshape(-1, chans)
    small_share, grad_input = after(sums[own:], grad_input)
    small = everywhere(small_share, small)
    grad_kernel = small[: TAPS * TAPS].reshape(dw_kernel.shape)
    return (
        block_out,
        grad_input,
        grad_fc1,
        grad_fc2,
        grad_kernel,
        small[TAPS * TAPS],
        small[TAPS * TAPS + 1],
    )


def solution(mesh):
    in_specs = (
        P("slide", None, "row", None, None),
        P("slide", None, "row", None, None),
        P("slide"),
        P(),
        P(),
        P(),
        P(),
        P(),
    )
    out_specs = (
        P("slide", None, "row", None, None),
        P("slide", None, "row", None, None),
        P(("slide", "row"), None),
        P(("slide", "row"), None),
        P(),
        P(),
        P(),
    )
    return jax.shard_map(body, mesh=mesh, in_specs=in_specs, out_specs=out_specs, check_vma=False)
```

```python
import itertools
import math

import jax
import jax.numpy as jnp
from jax import lax
from jax.experimental import pallas as pl
from jax.experimental.pallas import tpu as pltpu
from jax.sharding import PartitionSpec as P

epsilon = 1e-06
root_half = 1.0 / math.sqrt(2.0)
density = 1.0 / math.sqrt(2.0 * math.pi)
f32, bf16 = jnp.float32, jnp.bfloat16
REACH = 3
TAPS = 7
LEFT = 8
LANES = 128
MOST = 3
BLOCK = 768
SIDE = 4
PITCH = 24


def place(y, x, core, z):
    return ((y * SIDE + x) * 2 + core) * SIDE + z


def after(*values):
    return lax.optimization_barrier(values)


def from_other_core(half):
    return lax.ppermute(half, "slide", [(i, i ^ 1) for i in range(lax.axis_size("slide"))])


def quarters(mine, got):
    core = lax.axis_index("slide") % 2
    own = jnp.where(core == 0, lax.axis_index("row"), lax.axis_index("slide") // 2 % SIDE)

    def cut(half, by):
        cells = half.reshape(SIDE, SIDE, SIDE, -1, half.shape[-1])
        at = (own + by) % SIDE
        along_z = lax.dynamic_index_in_dim(cells, at, 2, keepdims=False)
        along_x = lax.dynamic_index_in_dim(cells, at, 1, keepdims=False)
        return jnp.where(core == 0, along_z, along_x).astype(f32)

    return [(cut(mine, by) + cut(got, by)).astype(bf16) for by in range(SIDE)]


def ring_sent(parts):
    every = [range(SIDE)] * 3
    pairs = [
        [
            move
            for y, x, z in itertools.product(*every)
            for move in (
                (place(y, x, 0, z), place(y, x, 0, (z + by) % SIDE)),
                (place(y, x, 1, z), place(y, (x + by) % SIDE, 1, z)),
            )
        ]
        for by in range(SIDE)
    ]
    return [lax.ppermute(parts[by], ("slide", "row"), pairs[by]) for by in range(1, SIDE)]


def total_of(own, got):
    total = own.astype(f32)
    for part in got:
        total = total + part.astype(f32)
    return total.astype(bf16).reshape(SIDE * SIDE, -1, own.shape[-1])


def plane_exchanged(blocks):
    every = [range(SIDE)] * 2
    groups = [[place(y, x, 0, z) for y, x in itertools.product(*every)] for z in range(SIDE)]
    groups += [[place(y, x, 1, z) for y, z in itertools.product(*every)] for x in range(SIDE)]
    got = lax.all_to_all(
        blocks.reshape(-1, blocks.shape[-1]),
        ("slide", "row"),
        0,
        0,
        axis_index_groups=groups,
        tiled=True,
    )
    return jnp.sum(got.reshape(blocks.shape).astype(f32), axis=0)


def everywhere(share):
    count = lax.axis_size("slide") * lax.axis_size("row")
    cells = share.astype(bf16).reshape(-1, LANES)
    sent = jnp.broadcast_to(cells[None], (count, *cells.shape))
    got = lax.all_to_all(sent, ("slide", "row"), 0, 0, tiled=True)
    got = got.reshape(SIDE, SIDE, 2, SIDE, *cells.shape).astype(f32)
    whole = jnp.sum(got[:, :, 0], axis=2) + jnp.sum(got[:, :, 1], axis=1)
    return whole.reshape(-1, share.shape[-1])


def edges(cells):
    ends = lax.axis_size("row") - 1
    head = cells[:, :REACH]
    tail = cells[:, cells.shape[1] - REACH :]
    above = lax.ppermute(tail, "row", [(i, i + 1) for i in range(ends)])
    below = lax.ppermute(head, "row", [(i + 1, i) for i in range(ends)])
    return above, below


def clear_padded(pad):
    pad[...] = jnp.zeros_like(pad)


def lane_blocks(chans, body):
    def step(i, carry):
        body(i, pl.ds(pl.multiple_of(i * LANES, LANES), LANES))
        return carry

    lax.fori_loop(0, chans // LANES, step, 0)


def fill_padded(pad, above, line_of, below, rows, cols, chans):
    def over(i, lanes):
        for r in range(REACH):
            pad[i, pl.ds(r * PITCH + LEFT, cols), :] = above[0, r, :, lanes].astype(f32)
            at = (rows + REACH + r) * PITCH + LEFT
            pad[i, pl.ds(at, cols), :] = below[0, r, :, lanes].astype(f32)
        for r in range(rows):
            pad[i, pl.ds((REACH + r) * PITCH + LEFT, cols), :] = line_of(r, lanes).astype(f32)

    lane_blocks(chans, over)


def window(pad, i, half, b, rows):
    shift = LEFT - REACH + b + 8 * half
    return [pad[i, pl.ds(r * PITCH + shift, 8), :] for r in range(rows + 2 * REACH)]


def stencil(pad, wide, rows, cols, chans, flip, emit):
    def over(i, lanes):
        for half in range(cols // 8):
            total = [None] * rows
            for b in range(TAPS):
                line = window(pad, i, half, b, rows)
                weights = []
                for a in range(TAPS):
                    tap = a * TAPS + b
                    weights.append(wide[TAPS * TAPS - 1 - tap if flip else tap, :, lanes])
                for p in range(rows):
                    m = [weights[a] * line[p + a] for a in range(TAPS)]
                    part = ((m[0] + m[1]) + (m[2] + m[3])) + ((m[4] + m[5]) + m[6])
                    total[p] = part if total[p] is None else total[p] + part
            for p in range(rows):
                emit(p, half, lanes, total[p])

    lane_blocks(chans, over)


def spread_kernel(wide, kernel_ref):
    for tap in range(TAPS * TAPS):
        wide[tap] = jnp.broadcast_to(kernel_ref[tap : tap + 1, :], wide.shape[1:])


def forward_kernel(
    count, tiles, above, below, cotan, kernel, gain, scale, normed, unit, spread, held_out, pad, wide, filt
):
    slot = pl.program_id(0)
    rows, cols, chans = tiles.shape[2:]

    @pl.when(slot == 0)
    def _():
        spread_kernel(wide, kernel)
        clear_padded(pad)

    def line_of(r, lanes):
        return tiles[0, 0, r, :, lanes]

    fill_padded(pad, above, line_of, below, rows, cols, chans)

    def emit(p, half, lanes, value):
        filt[pl.ds(p * cols + 8 * half, 8), lanes] = value

    stencil(pad, wide, rows, cols, chans, False, emit)
    weight = (slot < count[0]).astype(f32)
    held = cotan[...].reshape(rows * cols, chans).astype(f32) * weight
    held_out[...] = (held * scale[...]).astype(bf16)

    def norm(i, carry):
        at = pl.ds(pl.multiple_of(i * 64, 64), 64)
        value = filt[at, :]
        center = value - jnp.mean(value, axis=-1, keepdims=True)
        inv_std = lax.rsqrt(jnp.mean(center * center, axis=-1, keepdims=True) + epsilon)
        one = center * inv_std
        unit[at, :] = one
        normed[at, :] = (one * gain[...]).astype(bf16)
        spread[at, :] = jnp.broadcast_to(inv_std, (64, LANES))
        return carry

    lax.fori_loop(0, rows * cols // 64, norm, 0)


def gelu_parts(pre):
    size = jnp.abs(pre)
    bell = jnp.exp(pre * pre * -0.5)
    t = 1.0 / (1.0 + (0.3275911 * root_half) * size)
    poly = t * (
        0.5 * 0.254829592
        + t * (0.5 * -0.284496736 + t * (0.5 * 1.421413741 + t * (0.5 * -1.453152027 + t * (0.5 * 1.061405429))))
    )
    tail = poly * bell
    return jnp.where(pre < 0.0, tail, 1.0 - tail), bell * density


def hidden_kernel(core, normed, spread, first, act, slope, mine, other, turned, total):
    step = pl.program_id(0)

    @pl.when(step == 0)
    def _():
        turned[...] = spread[...].T

    pre = lax.dot_general(
        normed[...], first[...], (((1,), (1,)), ((), ())), preferred_element_type=f32
    )
    cdf, pdf = gelu_parts(pre)
    active = (pre * cdf).astype(bf16)
    act[...] = active
    slope[...] = (cdf + pre * pdf).astype(bf16)
    grad = jnp.dot(turned[...], active, preferred_element_type=f32)
    for i in range(BLOCK // LANES):
        total[i, pl.ds(step, grad.shape[0], stride=4), :] = grad[:, i * LANES : (i + 1) * LANES]

    @pl.when(step == pl.num_programs(0) - 1)
    def _():
        count = mine.shape[1]
        for chip in range(mine.shape[0]):
            for half, which in ((mine, core[0]), (other, 1 - core[0])):
                at = pl.ds(pl.multiple_of((2 * chip + which) * count, 32), count)
                for i in range(BLOCK // LANES):
                    half[chip, :, i * LANES : (i + 1) * LANES] = total[i, at, :].astype(bf16)


def back_kernel(
    core, normed, spread, slope, first, second, unit, inv, gain, mine, other, d_filt, gain_grad, total, term
):
    step = pl.program_id(0)
    pixels, chans = normed.shape
    d_act = jnp.dot(spread[...], second[...], preferred_element_type=f32)
    d_pre = (d_act * slope[...].astype(f32)).astype(bf16)
    term[...] = lax.dot_general(
        d_pre, normed[...], (((0,), (0,)), ((), ())), preferred_element_type=f32
    ).astype(bf16)
    d_normed = jnp.dot(d_pre, first[...], preferred_element_type=f32)
    count = mine.shape[1]
    for chip in range(mine.shape[0]):
        for half, which in ((mine, core[0]), (other, 1 - core[0])):
            at = pl.ds(pl.multiple_of((2 * chip + which) * count, 32), count)
            half[chip] = term[at, :]

    @pl.when(step == 0)
    def _():
        total[...] = d_normed

    @pl.when(step > 0)
    def _():
        total[...] += d_normed

    @pl.when(step == pl.num_programs(0) - 1)
    def _():
        def norm(i, kept):
            at = pl.ds(pl.multiple_of(i * 64, 64), 64)
            grad, one = total[at, :], unit[at, :]
            kept = kept + jnp.sum((grad * one).reshape(8, 8, chans), axis=0)
            scaled = grad * gain[...]
            mean = jnp.mean(scaled, axis=-1, keepdims=True)
            along = jnp.mean(scaled * one, axis=-1, keepdims=True)
            d_filt[at, :] = inv[at, 0:1] * (scaled - mean - one * along)
            return kept

        gain_grad[...] = lax.fori_loop(0, pixels // 64, norm, jnp.zeros((8, chans), f32))


def tap_kernel(tiles, above, below, d_filt, grad, pad, total):
    slot = pl.program_id(0)
    rows, cols, chans = tiles.shape[2:]

    @pl.when(slot == 0)
    def _():
        clear_padded(pad)
        total[...] = jnp.zeros_like(total)

    def line_of(r, lanes):
        return tiles[0, 0, r, :, lanes]

    fill_padded(pad, above, line_of, below, rows, cols, chans)

    def over(i, lanes):
        for half in range(cols // 8):
            back = [d_filt[pl.ds(p * cols + 8 * half, 8), lanes] for p in range(rows)]
            for b in range(TAPS):
                line = window(pad, i, half, b, rows)
                for a in range(TAPS):
                    m = [line[p + a] * back[p] for p in range(rows)]
                    while len(m) > 1:
                        m = [m[p] + m[p + 1] for p in range(0, len(m), 2)]
                    total[a * TAPS + b, :, lanes] += m[0]

    lane_blocks(chans, over)

    @pl.when(slot == pl.num_programs(0) - 1)
    def _():
        for tap in range(TAPS * TAPS):
            grad[tap : tap + 1, :] = jnp.sum(total[tap], axis=0, keepdims=True)


def input_kernel(count, d_filt, above, below, cotan, kernel, out, pad, wide):
    slot = pl.program_id(0)
    rows, cols, chans = out.shape[2:]

    @pl.when(slot == 0)
    def _():
        spread_kernel(wide, kernel)
        clear_padded(pad)

    @pl.when(slot < MOST)
    def _():
        def line_of(r, lanes):
            return d_filt[pl.ds(r * cols, cols), lanes]

        fill_padded(pad, above, line_of, below, rows, cols, chans)
        weight = (slot < count[0]).astype(f32)

        def emit(p, half, lanes, value):
            at = pl.ds(8 * half, 8)
            out[0, 0, p, at, lanes] = value + cotan[0, 0, p, at, lanes].astype(f32) * weight

        stencil(pad, wide, rows, cols, chans, True, emit)

    @pl.when(slot >= MOST)
    def _():
        out[...] = jnp.zeros_like(out)


def out_kernel(count, act, second, tiles, cotan, scale, out, scale_grad):
    slot = pl.program_id(0)
    rows, cols, chans = tiles.shape[2:]

    @pl.when(slot == 0)
    def _():
        scale_grad[...] = jnp.zeros_like(scale_grad)

    @pl.when(slot < count[0])
    def _():
        branch = lax.dot_general(
            act[...], second[...], (((1,), (1,)), ((), ())), preferred_element_type=f32
        )
        cells = tiles[...].reshape(rows * cols, chans).astype(f32)
        held = cotan[...].reshape(rows * cols, chans).astype(f32)
        scale_grad[...] += jnp.sum((held * branch).reshape(-1, 8, chans), axis=0)
        out[...] = (cells + scale[...] * branch).astype(bf16).reshape(out.shape)

    @pl.when(slot >= count[0])
    def _():
        out[...] = jnp.zeros_like(out)


def body(tiles, cotangent, tile_counts, dw_kernel, ln_gain, fc1_weight, fc2_weight, layer_scale):
    _, slots, rows, cols, chans = tiles.shape
    hidden = fc1_weight.shape[0]
    pixels = rows * cols
    every = MOST * pixels
    taps = dw_kernel.reshape(TAPS * TAPS, chans)
    gain, scale = ln_gain[None], layer_scale[None]
    above, below = edges(tiles[0, :MOST])

    params = pltpu.CompilerParams(
        vmem_limit_bytes=60 * 1024 * 1024, dimension_semantics=("arbitrary",)
    )
    shape = jax.ShapeDtypeStruct
    brief = pl.CostEstimate(flops=1, bytes_accessed=1, transcendentals=0)
    smem = pl.BlockSpec(memory_space=pltpu.SMEM)
    tile = pl.BlockSpec((1, 1, rows, cols, chans), lambda s: (0, s, 0, 0, 0))
    tile_live = pl.BlockSpec(
        (1, 1, rows, cols, chans), lambda s: (0, jnp.minimum(s, MOST - 1), 0, 0, 0)
    )
    edge = pl.BlockSpec((1, REACH, cols, chans), lambda s: (s, 0, 0, 0))
    edge_live = pl.BlockSpec(
        (1, REACH, cols, chans), lambda s: (jnp.minimum(s, MOST - 1), 0, 0, 0)
    )
    flat = pl.BlockSpec((pixels, chans), lambda s: (s, 0))
    flat_live = pl.BlockSpec((pixels, chans), lambda s: (jnp.minimum(s, MOST - 1), 0))

    def whole(*dims):
        return pl.BlockSpec(dims, lambda s: (0,) * len(dims))

    pad = pltpu.VMEM((chans // LANES, (rows + 2 * REACH) * PITCH + 8, LANES), f32)
    wide = pltpu.VMEM((TAPS * TAPS, 8, chans), f32)

    normed, unit, inv, spread = pl.pallas_call(
        forward_kernel,
        grid=(MOST,),
        in_specs=[smem, tile, edge, edge, tile, whole(TAPS * TAPS, chans), whole(1, chans), whole(1, chans)],
        out_specs=[flat, flat, pl.BlockSpec((pixels, LANES), lambda s: (s, 0)), flat],
        out_shape=[
            shape((every, chans), bf16),
            shape((every, chans), f32),
            shape((every, LANES), f32),
            shape((every, chans), bf16),
        ],
        scratch_shapes=[pad, wide, pltpu.VMEM((pixels, chans), f32)],
        compiler_params=params,
        cost_estimate=brief,
        name="forward",
    )(tile_counts, tiles, above, below, cotangent, taps, gain, scale)

    rows_of = pl.BlockSpec((BLOCK, chans), lambda j: (j, 0))
    cols_of = pl.BlockSpec((chans, BLOCK), lambda j: (0, j))
    wide_of = pl.BlockSpec((every, BLOCK), lambda j: (0, j))
    chips = SIDE * SIDE
    halves = shape((chips, hidden // (2 * chips), chans), bf16)
    core = (lax.axis_index("slide") % 2).reshape(1)
    act, slope, mine2, other2 = pl.pallas_call(
        hidden_kernel,
        grid=(hidden // BLOCK,),
        in_specs=[smem, whole(every, chans), whole(every, chans), rows_of],
        out_specs=[wide_of, wide_of, whole(*halves.shape), whole(*halves.shape)],
        out_shape=[shape((every, hidden), bf16), shape((every, hidden), bf16), halves, halves],
        scratch_shapes=[
            pltpu.VMEM((chans, every), bf16),
            pltpu.VMEM((chans // LANES, hidden, LANES), f32),
        ],
        compiler_params=params,
        cost_estimate=brief,
        name="hidden",
    )(core, normed, spread, fc1_weight)

    act, other2 = after(act, other2)
    got2 = from_other_core(other2)
    block_out, scale_grad = pl.pallas_call(
        out_kernel,
        grid=(slots,),
        in_specs=[
            smem,
            pl.BlockSpec((pixels, hidden), lambda s: (jnp.minimum(s, MOST - 1), 0)),
            whole(chans, hidden),
            tile_live,
            tile_live,
            whole(1, chans),
        ],
        out_specs=[tile, whole(8, chans)],
        out_shape=[shape(tiles.shape, bf16), shape((8, chans), f32)],
        compiler_params=params,
        cost_estimate=brief,
        name="outs",
    )(tile_counts, act, fc2_weight, tiles, cotangent, scale)

    mine2, got2, block_out = after(mine2, got2, block_out)
    parts2 = quarters(mine2, got2)
    slope, *parts2 = after(slope, *parts2)
    ring2 = ring_sent(parts2)

    quarter_of = pl.BlockSpec((SIDE, *halves.shape[1:]), lambda j: (j, 0, 0))
    mine1, other1, d_filt, gain_grad = pl.pallas_call(
        back_kernel,
        grid=(hidden // BLOCK,),
        in_specs=[
            smem,
            whole(every, chans),
            whole(every, chans),
            wide_of,
            rows_of,
            cols_of,
            whole(every, chans),
            whole(every, LANES),
            whole(1, chans),
        ],
        out_specs=[quarter_of, quarter_of, whole(every, chans), whole(8, chans)],
        out_shape=[halves, halves, shape((every, chans), f32), shape((8, chans), f32)],
        scratch_shapes=[pltpu.VMEM((every, chans), f32), pltpu.VMEM((BLOCK, chans), bf16)],
        compiler_params=params,
        cost_estimate=brief,
        name="back",
    )(core, normed, spread, slope, fc1_weight, fc2_weight, unit, inv, gain)

    sum2 = total_of(parts2[0], ring2)
    other1, sum2 = after(other1, sum2)
    got1 = from_other_core(other1)
    d_cells = d_filt.reshape(MOST, rows, cols, chans)
    d_above, d_below = edges(d_cells.astype(bf16))
    parts1 = quarters(mine1, got1)
    d_filt, *parts1 = after(d_filt, *parts1)
    ring1 = ring_sent(parts1)

    tap_grad = pl.pallas_call(
        tap_kernel,
        grid=(MOST,),
        in_specs=[tile, edge, edge, flat],
        out_specs=whole(TAPS * TAPS, chans),
        out_shape=shape((TAPS * TAPS, chans), f32),
        scratch_shapes=[pad, wide],
        compiler_params=params,
        cost_estimate=brief,
        name="taps",
    )(tiles, above, below, d_filt)

    scale_row = jnp.sum(scale_grad, axis=0)
    gain_row = jnp.sum(gain_grad, axis=0)
    small = jnp.concatenate([tap_grad, gain_row[None], scale_row[None]]).astype(bf16)
    lines = -(-small.shape[0] // chips)
    small = jnp.pad(small, ((0, chips * lines - small.shape[0]), (0, 0)))
    small = jnp.pad(small.reshape(chips, lines, chans), ((0, 0), (0, -lines % 8), (0, 0)))
    blocks = jnp.concatenate([sum2, total_of(parts1[0], ring1), small], axis=1)
    blocks, d_above, d_below, d_filt = after(blocks, d_above, d_below, d_filt)
    sums = plane_exchanged(blocks)

    grad_input = pl.pallas_call(
        input_kernel,
        grid=(slots,),
        in_specs=[smem, flat_live, edge_live, edge_live, tile_live, whole(TAPS * TAPS, chans)],
        out_specs=tile,
        out_shape=shape(tiles.shape, f32),
        scratch_shapes=[pad, wide],
        compiler_params=params,
        cost_estimate=brief,
        name="inputs",
    )(tile_counts, d_filt, d_above, d_below, cotangent, taps)

    own = hidden // (8 * chips)
    grad_fc2 = sums[:own].reshape(-1, hidden)
    grad_fc1 = sums[own : 2 * own]
    share, grad_input = after(sums[2 * own : 2 * own + lines], grad_input)
    small = everywhere(share)
    grad_kernel = small[: TAPS * TAPS].reshape(dw_kernel.shape)
    return (
        block_out,
        grad_input,
        grad_fc1,
        grad_fc2,
        grad_kernel,
        small[TAPS * TAPS],
        small[TAPS * TAPS + 1],
    )


def solution(mesh):
    in_specs = (
        P("slide", None, "row", None, None),
        P("slide", None, "row", None, None),
        P("slide"),
        P(),
        P(),
        P(),
        P(),
        P(),
    )
    out_specs = (
        P("slide", None, "row", None, None),
        P("slide", None, "row", None, None),
        P(("slide", "row"), None),
        P(("slide", "row"), None),
        P(),
        P(),
        P(),
    )
    return jax.shard_map(body, mesh=mesh, in_specs=in_specs, out_specs=out_specs, check_vma=False)
```

```python
import itertools
import math

import jax
import jax.numpy as jnp
from jax import lax
from jax.experimental import pallas as pl
from jax.experimental.pallas import tpu as pltpu
from jax.sharding import PartitionSpec as P

epsilon = 1e-06
root_half = 1.0 / math.sqrt(2.0)
density = 1.0 / math.sqrt(2.0 * math.pi)
f32, bf16 = jnp.float32, jnp.bfloat16
REACH = 3
TAPS = 7
LEFT = 8
LANES = 128
MOST = 3
BLOCK = 768
SIDE = 4
PITCH = 24


def place(y, x, core, z):
    return ((y * SIDE + x) * 2 + core) * SIDE + z


def after(*values):
    return lax.optimization_barrier(values)


def from_other_core(half):
    return lax.ppermute(half, "slide", [(i, i ^ 1) for i in range(lax.axis_size("slide"))])


def quarters(mine, got):
    core = lax.axis_index("slide") % 2
    own = jnp.where(core == 0, lax.axis_index("row"), lax.axis_index("slide") // 2 % SIDE)

    def cut(half, by):
        cells = half.reshape(SIDE, SIDE, SIDE, -1, half.shape[-1])
        at = (own + by) % SIDE
        along_z = lax.dynamic_index_in_dim(cells, at, 2, keepdims=False)
        along_x = lax.dynamic_index_in_dim(cells, at, 1, keepdims=False)
        return jnp.where(core == 0, along_z, along_x).astype(f32)

    return [(cut(mine, by) + cut(got, by)).astype(bf16) for by in range(SIDE)]


def ring_sent(parts):
    every = [range(SIDE)] * 3
    pairs = [
        [
            move
            for y, x, z in itertools.product(*every)
            for move in (
                (place(y, x, 0, z), place(y, x, 0, (z + by) % SIDE)),
                (place(y, x, 1, z), place(y, (x + by) % SIDE, 1, z)),
            )
        ]
        for by in range(SIDE)
    ]
    return [lax.ppermute(parts[by], ("slide", "row"), pairs[by]) for by in range(1, SIDE)]


def total_of(own, got):
    total = own.astype(f32)
    for part in got:
        total = total + part.astype(f32)
    return total.astype(bf16).reshape(SIDE * SIDE, -1, own.shape[-1])


def plane_exchanged(blocks):
    every = [range(SIDE)] * 2
    groups = [[place(y, x, 0, z) for y, x in itertools.product(*every)] for z in range(SIDE)]
    groups += [[place(y, x, 1, z) for y, z in itertools.product(*every)] for x in range(SIDE)]
    got = lax.all_to_all(
        blocks.reshape(-1, blocks.shape[-1]),
        ("slide", "row"),
        0,
        0,
        axis_index_groups=groups,
        tiled=True,
    )
    return jnp.sum(got.reshape(blocks.shape).astype(f32), axis=0)


def everywhere(share):
    count = lax.axis_size("slide") * lax.axis_size("row")
    cells = share.astype(bf16).reshape(-1, LANES)
    sent = jnp.broadcast_to(cells[None], (count, *cells.shape))
    got = lax.all_to_all(sent, ("slide", "row"), 0, 0, tiled=True)
    got = got.reshape(SIDE, SIDE, 2, SIDE, *cells.shape).astype(f32)
    whole = jnp.sum(got[:, :, 0], axis=2) + jnp.sum(got[:, :, 1], axis=1)
    return whole.reshape(-1, share.shape[-1])


def edges(cells):
    ends = lax.axis_size("row") - 1
    head = cells[:, :REACH]
    tail = cells[:, cells.shape[1] - REACH :]
    above = lax.ppermute(tail, "row", [(i, i + 1) for i in range(ends)])
    below = lax.ppermute(head, "row", [(i + 1, i) for i in range(ends)])
    return above, below


def clear_padded(pad):
    pad[...] = jnp.zeros_like(pad)


def lane_blocks(chans, body):
    def step(i, carry):
        body(i, pl.ds(pl.multiple_of(i * LANES, LANES), LANES))
        return carry

    lax.fori_loop(0, chans // LANES, step, 0)


def fill_padded(pad, above, line_of, below, rows, cols, chans):
    def over(i, lanes):
        for r in range(REACH):
            pad[i, pl.ds(r * PITCH + LEFT, cols), :] = above[0, r, :, lanes].astype(f32)
            at = (rows + REACH + r) * PITCH + LEFT
            pad[i, pl.ds(at, cols), :] = below[0, r, :, lanes].astype(f32)
        for r in range(rows):
            pad[i, pl.ds((REACH + r) * PITCH + LEFT, cols), :] = line_of(r, lanes).astype(f32)

    lane_blocks(chans, over)


def window(pad, i, half, b, rows):
    shift = LEFT - REACH + b + 8 * half
    return [pad[i, pl.ds(r * PITCH + shift, 8), :] for r in range(rows + 2 * REACH)]


def stencil(pad, wide, rows, cols, chans, flip, emit):
    def over(i, lanes):
        for half in range(cols // 8):
            total = [None] * rows
            for b in range(TAPS):
                line = window(pad, i, half, b, rows)
                weights = []
                for a in range(TAPS):
                    tap = a * TAPS + b
                    weights.append(wide[TAPS * TAPS - 1 - tap if flip else tap, :, lanes])
                for p in range(rows):
                    m = [weights[a] * line[p + a] for a in range(TAPS)]
                    part = ((m[0] + m[1]) + (m[2] + m[3])) + ((m[4] + m[5]) + m[6])
                    total[p] = part if total[p] is None else total[p] + part
            for p in range(rows):
                emit(p, half, lanes, total[p])

    lane_blocks(chans, over)


def spread_kernel(wide, kernel_ref):
    for tap in range(TAPS * TAPS):
        wide[tap] = jnp.broadcast_to(kernel_ref[tap : tap + 1, :], wide.shape[1:])


def forward_kernel(
    count, tiles, above, below, cotan, kernel, gain, scale, normed, unit, spread, held_out, pad, wide, filt
):
    slot = pl.program_id(0)
    rows, cols, chans = tiles.shape[2:]

    @pl.when(slot == 0)
    def _():
        spread_kernel(wide, kernel)
        clear_padded(pad)

    def line_of(r, lanes):
        return tiles[0, 0, r, :, lanes]

    fill_padded(pad, above, line_of, below, rows, cols, chans)

    def emit(p, half, lanes, value):
        filt[pl.ds(p * cols + 8 * half, 8), lanes] = value

    stencil(pad, wide, rows, cols, chans, False, emit)
    weight = (slot < count[0]).astype(f32)
    held = cotan[...].reshape(rows * cols, chans).astype(f32) * weight
    held_out[...] = (held * scale[...]).astype(bf16)

    def norm(i, carry):
        at = pl.ds(pl.multiple_of(i * 64, 64), 64)
        value = filt[at, :]
        center = value - jnp.mean(value, axis=-1, keepdims=True)
        inv_std = lax.rsqrt(jnp.mean(center * center, axis=-1, keepdims=True) + epsilon)
        one = center * inv_std
        unit[at, :] = one
        normed[at, :] = (one * gain[...]).astype(bf16)
        spread[at, :] = jnp.broadcast_to(inv_std, (64, LANES))
        return carry

    lax.fori_loop(0, rows * cols // 64, norm, 0)


def gelu_parts(pre):
    size = jnp.abs(pre)
    bell = jnp.exp(pre * pre * -0.5)
    t = 1.0 / (1.0 + (0.3275911 * root_half) * size)
    poly = t * (
        0.5 * 0.254829592
        + t * (0.5 * -0.284496736 + t * (0.5 * 1.421413741 + t * (0.5 * -1.453152027 + t * (0.5 * 1.061405429))))
    )
    tail = poly * bell
    return jnp.where(pre < 0.0, tail, 1.0 - tail), bell * density


def split_rows(core, mine, other, rows_at):
    count = mine.shape[1]
    for chip in range(mine.shape[0]):
        for half, which in ((mine, core[0]), (other, 1 - core[0])):
            rows_at(half, chip, pl.ds(pl.multiple_of((2 * chip + which) * count, 32), count))


def mlp_kernel(
    core, count, normed, spread, first, second, unit, inv, gain, scale, tiles, cotan,
    mine1, other1, mine2, other2, d_filt, out, gain_grad, scale_grad,
    turned, total2, term, back, branch,
):
    step = pl.program_id(0)
    pixels, chans = normed.shape
    rows, cols = tiles.shape[2:4]

    @pl.when(step == 0)
    def _():
        turned[...] = spread[...].T
        back[...] = jnp.zeros_like(back)
        branch[...] = jnp.zeros_like(branch)

    pre = lax.dot_general(
        normed[...], first[...], (((1,), (1,)), ((), ())), preferred_element_type=f32
    )
    d_act = jnp.dot(spread[...], second[...], preferred_element_type=f32)
    cdf, pdf = gelu_parts(pre)
    active = (pre * cdf).astype(bf16)
    d_pre = (d_act * (cdf + pre * pdf)).astype(bf16)
    grad = jnp.dot(turned[...], active, preferred_element_type=f32)
    for i in range(BLOCK // LANES):
        total2[i, pl.ds(step, chans, stride=4), :] = grad[:, i * LANES : (i + 1) * LANES]
    branch[...] += lax.dot_general(
        active, second[...], (((1,), (1,)), ((), ())), preferred_element_type=f32
    )
    term[...] = lax.dot_general(
        d_pre, normed[...], (((0,), (0,)), ((), ())), preferred_element_type=f32
    ).astype(bf16)

    def copy1(half, chip, at):
        half[chip] = term[at, :]

    split_rows(core, mine1, other1, copy1)
    back[...] += jnp.dot(d_pre, first[...], preferred_element_type=f32)

    @pl.when(step == pl.num_programs(0) - 1)
    def _():
        def copy2(half, chip, at):
            for i in range(BLOCK // LANES):
                half[chip, :, i * LANES : (i + 1) * LANES] = total2[i, at, :].astype(bf16)

        split_rows(core, mine2, other2, copy2)
        lines = 64 // cols

        def finish(i, kept):
            gains, scales = kept
            at = pl.ds(pl.multiple_of(i * 64, 64), 64)
            grad, one = back[at, :], unit[at, :]
            gains = gains + jnp.sum((grad * one).reshape(8, 8, chans), axis=0)
            scaled = grad * gain[...]
            mean = jnp.mean(scaled, axis=-1, keepdims=True)
            along = jnp.mean(scaled * one, axis=-1, keepdims=True)
            d_filt[at, :] = inv[at, 0:1] * (scaled - mean - one * along)
            slot = i * lines // rows
            weight = (slot < count[0]).astype(f32)
            line = pl.ds(i * lines - slot * rows, lines)
            value = branch[at, :]
            held = cotan[0, slot, line].reshape(64, chans).astype(f32) * weight
            scales = scales + jnp.sum((held * value).reshape(8, 8, chans), axis=0)
            cells = tiles[0, slot, line].reshape(64, chans).astype(f32)
            filled = ((cells + scale[...] * value) * weight).astype(bf16)
            out[0, slot, line] = filled.reshape(lines, cols, chans)
            return gains, scales

        start = jnp.zeros((8, chans), f32)
        gain_grad[...], scale_grad[...] = lax.fori_loop(0, pixels // 64, finish, (start, start))
        out[0, MOST:] = jnp.zeros((out.shape[1] - MOST, rows, cols, chans), bf16)


def tap_kernel(tiles, above, below, d_filt, grad, pad, total):
    slot = pl.program_id(0)
    rows, cols, chans = tiles.shape[2:]

    @pl.when(slot == 0)
    def _():
        clear_padded(pad)
        total[...] = jnp.zeros_like(total)

    def line_of(r, lanes):
        return tiles[0, 0, r, :, lanes]

    fill_padded(pad, above, line_of, below, rows, cols, chans)

    def over(i, lanes):
        for half in range(cols // 8):
            back = [d_filt[pl.ds(p * cols + 8 * half, 8), lanes] for p in range(rows)]
            for b in range(TAPS):
                line = window(pad, i, half, b, rows)
                for a in range(TAPS):
                    m = [line[p + a] * back[p] for p in range(rows)]
                    while len(m) > 1:
                        m = [m[p] + m[p + 1] for p in range(0, len(m), 2)]
                    total[a * TAPS + b, :, lanes] += m[0]

    lane_blocks(chans, over)

    @pl.when(slot == pl.num_programs(0) - 1)
    def _():
        for tap in range(TAPS * TAPS):
            grad[tap : tap + 1, :] = jnp.sum(total[tap], axis=0, keepdims=True)


def input_kernel(count, d_filt, above, below, cotan, kernel, out, pad, wide):
    slot = pl.program_id(0)
    rows, cols, chans = out.shape[2:]

    @pl.when(slot == 0)
    def _():
        spread_kernel(wide, kernel)
        clear_padded(pad)

    @pl.when(slot < MOST)
    def _():
        def line_of(r, lanes):
            return d_filt[pl.ds(r * cols, cols), lanes]

        fill_padded(pad, above, line_of, below, rows, cols, chans)
        weight = (slot < count[0]).astype(f32)

        def emit(p, half, lanes, value):
            at = pl.ds(8 * half, 8)
            out[0, 0, p, at, lanes] = value + cotan[0, 0, p, at, lanes].astype(f32) * weight

        stencil(pad, wide, rows, cols, chans, True, emit)

    @pl.when(slot >= MOST)
    def _():
        out[...] = jnp.zeros_like(out)


def body(tiles, cotangent, tile_counts, dw_kernel, ln_gain, fc1_weight, fc2_weight, layer_scale):
    _, slots, rows, cols, chans = tiles.shape
    hidden = fc1_weight.shape[0]
    pixels = rows * cols
    every = MOST * pixels
    taps = dw_kernel.reshape(TAPS * TAPS, chans)
    gain, scale = ln_gain[None], layer_scale[None]
    above, below = edges(tiles[0, :MOST])

    params = pltpu.CompilerParams(
        vmem_limit_bytes=60 * 1024 * 1024, dimension_semantics=("arbitrary",)
    )
    shape = jax.ShapeDtypeStruct
    brief = pl.CostEstimate(flops=1, bytes_accessed=1, transcendentals=0)
    smem = pl.BlockSpec(memory_space=pltpu.SMEM)
    tile = pl.BlockSpec((1, 1, rows, cols, chans), lambda s: (0, s, 0, 0, 0))
    tile_live = pl.BlockSpec(
        (1, 1, rows, cols, chans), lambda s: (0, jnp.minimum(s, MOST - 1), 0, 0, 0)
    )
    edge = pl.BlockSpec((1, REACH, cols, chans), lambda s: (s, 0, 0, 0))
    edge_live = pl.BlockSpec(
        (1, REACH, cols, chans), lambda s: (jnp.minimum(s, MOST - 1), 0, 0, 0)
    )
    flat = pl.BlockSpec((pixels, chans), lambda s: (s, 0))
    flat_live = pl.BlockSpec((pixels, chans), lambda s: (jnp.minimum(s, MOST - 1), 0))

    def whole(*dims):
        return pl.BlockSpec(dims, lambda s: (0,) * len(dims))

    pad = pltpu.VMEM((chans // LANES, (rows + 2 * REACH) * PITCH + 8, LANES), f32)
    wide = pltpu.VMEM((TAPS * TAPS, 8, chans), f32)

    normed, unit, inv, spread = pl.pallas_call(
        forward_kernel,
        grid=(MOST,),
        in_specs=[smem, tile, edge, edge, tile, whole(TAPS * TAPS, chans), whole(1, chans), whole(1, chans)],
        out_specs=[flat, flat, pl.BlockSpec((pixels, LANES), lambda s: (s, 0)), flat],
        out_shape=[
            shape((every, chans), bf16),
            shape((every, chans), f32),
            shape((every, LANES), f32),
            shape((every, chans), bf16),
        ],
        scratch_shapes=[pad, wide, pltpu.VMEM((pixels, chans), f32)],
        compiler_params=params,
        cost_estimate=brief,
        name="forward",
    )(tile_counts, tiles, above, below, cotangent, taps, gain, scale)

    chips = SIDE * SIDE
    halves = shape((chips, hidden // (2 * chips), chans), bf16)
    core = (lax.axis_index("slide") % 2).reshape(1)

    def once(*dims):
        return pl.BlockSpec(dims, lambda s: (0,) * len(dims), pipeline_mode=pl.Buffered(1))

    quarter_of = pl.BlockSpec((SIDE, *halves.shape[1:]), lambda j: (j, 0, 0))
    live = once(1, MOST, rows, cols, chans)
    mine1, other1, mine2, other2, d_filt, block_out, gain_grad, scale_grad = pl.pallas_call(
        mlp_kernel,
        grid=(hidden // BLOCK,),
        in_specs=[
            smem,
            smem,
            once(every, chans),
            once(every, chans),
            pl.BlockSpec((BLOCK, chans), lambda j: (j, 0)),
            pl.BlockSpec((chans, BLOCK), lambda j: (0, j)),
            once(every, chans),
            once(every, LANES),
            once(1, chans),
            once(1, chans),
            live,
            live,
        ],
        out_specs=[
            quarter_of,
            quarter_of,
            once(*halves.shape),
            once(*halves.shape),
            once(every, chans),
            once(*tiles.shape),
            once(8, chans),
            once(8, chans),
        ],
        out_shape=[
            halves,
            halves,
            halves,
            halves,
            shape((every, chans), f32),
            shape(tiles.shape, bf16),
            shape((8, chans), f32),
            shape((8, chans), f32),
        ],
        scratch_shapes=[
            pltpu.VMEM((chans, every), bf16),
            pltpu.VMEM((chans // LANES, hidden, LANES), f32),
            pltpu.VMEM((BLOCK, chans), bf16),
            pltpu.VMEM((every, chans), f32),
            pltpu.VMEM((every, chans), f32),
        ],
        compiler_params=params,
        cost_estimate=brief,
        name="mlp",
    )(
        core, tile_counts, normed, spread, fc1_weight, fc2_weight, unit, inv, gain, scale, tiles, cotangent
    )

    got2, got1 = from_other_core(other2), from_other_core(other1)
    d_cells = d_filt.reshape(MOST, rows, cols, chans)
    d_above, d_below = edges(d_cells.astype(bf16))

    tap_grad = pl.pallas_call(
        tap_kernel,
        grid=(MOST,),
        in_specs=[tile, edge, edge, flat],
        out_specs=whole(TAPS * TAPS, chans),
        out_shape=shape((TAPS * TAPS, chans), f32),
        scratch_shapes=[pad, wide],
        compiler_params=params,
        cost_estimate=brief,
        name="taps",
    )(tiles, above, below, d_filt)

    scale_row = jnp.sum(scale_grad, axis=0)
    gain_row = jnp.sum(gain_grad, axis=0)
    small = jnp.concatenate([tap_grad, gain_row[None], scale_row[None]]).astype(bf16)
    lines = -(-small.shape[0] // chips)
    small = jnp.pad(small, ((0, chips * lines - small.shape[0]), (0, 0)))
    small = jnp.pad(small.reshape(chips, lines, chans), ((0, 0), (0, -lines % 8), (0, 0)))
    small, d_above, d_below, mine1, got1, mine2, got2 = after(
        small, d_above, d_below, mine1, got1, mine2, got2
    )
    share = plane_exchanged(small)[:lines]
    parts = quarters(mine2, got2) + quarters(mine1, got1)
    ring2, ring1 = ring_sent(parts[:SIDE]), ring_sent(parts[SIDE:])
    share, _, _ = after(share, parts[SIDE - 1], parts[-1])
    share, d_filt, d_above, d_below = after(share, d_filt, d_above, d_below)
    small = everywhere(share)

    grad_input = pl.pallas_call(
        input_kernel,
        grid=(slots,),
        in_specs=[smem, flat_live, edge_live, edge_live, tile_live, whole(TAPS * TAPS, chans)],
        out_specs=tile,
        out_shape=shape(tiles.shape, f32),
        scratch_shapes=[pad, wide],
        compiler_params=params,
        cost_estimate=brief,
        name="inputs",
    )(tile_counts, d_filt, d_above, d_below, cotangent, taps)

    grad_kernel = small[: TAPS * TAPS].reshape(dw_kernel.shape)
    blocks = jnp.concatenate([total_of(parts[0], ring2), total_of(parts[SIDE], ring1)], axis=1)
    blocks, small, grad_input = after(blocks, small, grad_input)
    sums = plane_exchanged(blocks)
    own = hidden // (8 * chips)
    grad_fc2 = sums[:own].reshape(-1, hidden)
    grad_fc1 = sums[own:]
    return (
        block_out,
        grad_input,
        grad_fc1,
        grad_fc2,
        grad_kernel,
        small[TAPS * TAPS],
        small[TAPS * TAPS + 1],
    )


def solution(mesh):
    in_specs = (
        P("slide", None, "row", None, None),
        P("slide", None, "row", None, None),
        P("slide"),
        P(),
        P(),
        P(),
        P(),
        P(),
    )
    out_specs = (
        P("slide", None, "row", None, None),
        P("slide", None, "row", None, None),
        P(("slide", "row"), None),
        P(("slide", "row"), None),
        P(),
        P(),
        P(),
    )
    return jax.shard_map(body, mesh=mesh, in_specs=in_specs, out_specs=out_specs, check_vma=False)
```

```python
import itertools
import math

import jax
import jax.numpy as jnp
from jax import lax
from jax.experimental import pallas as pl
from jax.experimental.pallas import tpu as pltpu
from jax.sharding import PartitionSpec as P

epsilon = 1e-06
root_half = 1.0 / math.sqrt(2.0)
density = 1.0 / math.sqrt(2.0 * math.pi)
f32, bf16 = jnp.float32, jnp.bfloat16
REACH = 3
TAPS = 7
LEFT = 8
LANES = 128
WORK = 2
BLOCK = 768
SIDE = 4
PITCH = 24


def place(y, x, core, z):
    return ((y * SIDE + x) * 2 + core) * SIDE + z


def after(*values):
    return lax.optimization_barrier(values)


def from_other_core(half):
    return lax.ppermute(half, "slide", [(i, i ^ 1) for i in range(lax.axis_size("slide"))])


def quarters(mine, got):
    core = lax.axis_index("slide") % 2
    own = jnp.where(core == 0, lax.axis_index("row"), lax.axis_index("slide") // 2 % SIDE)

    def cut(half, by):
        return lax.dynamic_index_in_dim(half, (own + by) % SIDE, 0, keepdims=False).astype(f32)

    return [(cut(mine, by) + cut(got, by)).astype(bf16) for by in range(SIDE)]


def ring_sent(parts):
    every = [range(SIDE)] * 3
    pairs = [
        [
            move
            for y, x, z in itertools.product(*every)
            for move in (
                (place(y, x, 0, z), place(y, x, 0, (z + by) % SIDE)),
                (place(y, x, 1, z), place(y, (x + by) % SIDE, 1, z)),
            )
        ]
        for by in range(SIDE)
    ]
    return [lax.ppermute(parts[by], ("slide", "row"), pairs[by]) for by in range(1, SIDE)]


def total_of(own, got):
    total = own.astype(f32)
    for part in got:
        total = total + part.astype(f32)
    return total.astype(bf16).reshape(SIDE * SIDE, -1, own.shape[-1])


def plane_exchanged(blocks):
    every = [range(SIDE)] * 2
    groups = [[place(y, x, 0, z) for y, x in itertools.product(*every)] for z in range(SIDE)]
    groups += [[place(y, x, 1, z) for y, z in itertools.product(*every)] for x in range(SIDE)]
    got = lax.all_to_all(
        blocks.reshape(-1, blocks.shape[-1]),
        ("slide", "row"),
        0,
        0,
        axis_index_groups=groups,
        tiled=True,
    )
    return jnp.sum(got.reshape(blocks.shape).astype(f32), axis=0)


def everywhere(share):
    count = lax.axis_size("slide") * lax.axis_size("row")
    cells = share.astype(bf16).reshape(-1, LANES)
    sent = jnp.broadcast_to(cells[None], (count, *cells.shape))
    got = lax.all_to_all(sent, ("slide", "row"), 0, 0, tiled=True)
    got = got.reshape(SIDE, SIDE, 2, SIDE, *cells.shape).astype(f32)
    whole = jnp.sum(got[:, :, 0], axis=2) + jnp.sum(got[:, :, 1], axis=1)
    return whole.reshape(-1, share.shape[-1])


def edges(head, tail):
    ends = lax.axis_size("row") - 1
    above = lax.ppermute(tail, "row", [(i, i + 1) for i in range(ends)])
    below = lax.ppermute(head, "row", [(i + 1, i) for i in range(ends)])
    return above, below


def clear_padded(pad):
    pad[...] = jnp.zeros_like(pad)


def lane_blocks(chans, body):
    def step(i, carry):
        body(i, pl.ds(pl.multiple_of(i * LANES, LANES), LANES))
        return carry

    lax.fori_loop(0, chans // LANES, step, 0)


def fill_padded(pad, above, line_of, below, rows, cols, chans):
    def over(i, lanes):
        for r in range(REACH):
            pad[i, pl.ds(r * PITCH + LEFT, cols), :] = above[0, r, :, lanes].astype(f32)
            at = (rows + REACH + r) * PITCH + LEFT
            pad[i, pl.ds(at, cols), :] = below[0, r, :, lanes].astype(f32)
        for r in range(rows):
            pad[i, pl.ds((REACH + r) * PITCH + LEFT, cols), :] = line_of(r, lanes).astype(f32)

    lane_blocks(chans, over)


def window(pad, i, half, b, rows):
    shift = LEFT - REACH + b + 8 * half
    return [pad[i, pl.ds(r * PITCH + shift, 8), :] for r in range(rows + 2 * REACH)]


def stencil(pad, wide, rows, cols, chans, flip, emit):
    def over(i, lanes):
        for half in range(cols // 8):
            total = [None] * rows
            for b in range(TAPS):
                line = window(pad, i, half, b, rows)
                weights = []
                for a in range(TAPS):
                    tap = a * TAPS + b
                    weights.append(wide[TAPS * TAPS - 1 - tap if flip else tap, :, lanes])
                for p in range(rows):
                    m = [weights[a] * line[p + a] for a in range(TAPS)]
                    part = ((m[0] + m[1]) + (m[2] + m[3])) + ((m[4] + m[5]) + m[6])
                    total[p] = part if total[p] is None else total[p] + part
            for p in range(rows):
                emit(p, half, lanes, total[p])

    lane_blocks(chans, over)


def spread_kernel(wide, kernel_ref):
    for tap in range(TAPS * TAPS):
        wide[tap] = jnp.broadcast_to(kernel_ref[tap : tap + 1, :], wide.shape[1:])


def forward_kernel(
    tiles, above, below, cotan, kernel, gain, scale, *refs
):
    normed, unit, spread, held_out, pad, wide, filt = refs[-7:]
    rows, cols, chans = tiles.shape[1:]
    spread_kernel(wide, kernel)
    clear_padded(pad)

    def line_of(r, lanes):
        return tiles[0, r, :, lanes]

    fill_padded(pad, above, line_of, below, rows, cols, chans)

    def emit(p, half, lanes, value):
        filt[pl.ds(p * cols + 8 * half, 8), lanes] = value

    stencil(pad, wide, rows, cols, chans, False, emit)
    held = cotan[...].reshape(rows * cols, chans).astype(f32)
    held_out[...] = (held * scale[...]).astype(bf16)

    def norm(i, carry):
        at = pl.ds(pl.multiple_of(i * 64, 64), 64)
        value = filt[at, :]
        center = value - jnp.mean(value, axis=-1, keepdims=True)
        inv_std = lax.rsqrt(jnp.mean(center * center, axis=-1, keepdims=True) + epsilon)
        one = center * inv_std
        unit[at, :] = one
        normed[at, :] = (one * gain[...]).astype(bf16)
        spread[at, :] = jnp.broadcast_to(inv_std, (64, LANES))
        return carry

    lax.fori_loop(0, rows * cols // 64, norm, 0)


def gelu_parts(pre):
    size = jnp.abs(pre)
    bell = jnp.exp(pre * pre * -0.5)
    t = 1.0 / (1.0 + (0.3275911 * root_half) * size)
    poly = t * (
        0.5 * 0.254829592
        + t * (0.5 * -0.284496736 + t * (0.5 * 1.421413741 + t * (0.5 * -1.453152027 + t * (0.5 * 1.061405429))))
    )
    tail = poly * bell
    return jnp.where(pre < 0.0, tail, 1.0 - tail), bell * density


def split_rows(core, mine, other, y, first, rows_at):
    count = mine.shape[3]
    for x, z in itertools.product(range(SIDE), repeat=2):
        flipped = [jnp.where(core[0] == 0, *pair) for pair in ((z, x), (x, z))]
        for half, which, at in ((mine, core[0], flipped), (other, 1 - core[0], flipped[::-1])):
            begin = pl.multiple_of(first + ((2 * x + which) * SIDE + z) * count, 8)
            rows_at(half, (at[0], y, at[1]), pl.ds(begin, count))


def mlp_kernel(
    core, normed, spread, first, second, unit, inv, gain, scale, tiles, cotan,
    mine1, other1, mine2, other2, d_filt, d_head, d_tail, out, gain_grad, scale_grad,
    turned, total2, term, back, branch,
):
    step = pl.program_id(0)
    pixels, chans = normed.shape
    rows, cols = tiles.shape[1:3]

    @pl.when(step == 0)
    def _():
        turned[...] = spread[...].T
        back[...] = jnp.zeros_like(back)
        branch[...] = jnp.zeros_like(branch)

    pre = lax.dot_general(
        normed[...], first[...], (((1,), (1,)), ((), ())), preferred_element_type=f32
    )
    d_act = jnp.dot(spread[...], second[...], preferred_element_type=f32)
    cdf, pdf = gelu_parts(pre)
    active = (pre * cdf).astype(bf16)
    d_pre = (d_act * (cdf + pre * pdf)).astype(bf16)
    grad = jnp.dot(turned[...], active, preferred_element_type=f32)
    for i in range(BLOCK // LANES):
        total2[i, pl.ds(step, chans, stride=4), :] = grad[:, i * LANES : (i + 1) * LANES]
    branch[...] += lax.dot_general(
        active, second[...], (((1,), (1,)), ((), ())), preferred_element_type=f32
    )
    term[...] = lax.dot_general(
        d_pre, normed[...], (((0,), (0,)), ((), ())), preferred_element_type=f32
    )

    def copy1(half, chip, at):
        half[chip] = term[at, :].astype(bf16)

    split_rows(core, mine1, other1, 0, 0, copy1)
    back[...] += jnp.dot(d_pre, first[...], preferred_element_type=f32)

    @pl.when(step == pl.num_programs(0) - 1)
    def _():
        def copy2(half, chip, at):
            for i in range(BLOCK // LANES):
                lanes = slice(i * LANES, (i + 1) * LANES)
                half[(*chip, slice(None), lanes)] = total2[i, at, :].astype(bf16)

        def over(y, carry):
            split_rows(core, mine2, other2, y, y * (total2.shape[1] // SIDE), copy2)
            return carry

        lax.fori_loop(0, SIDE, over, 0)
        lines = 64 // cols

        def finish(i, kept):
            gains, scales = kept
            at = pl.ds(pl.multiple_of(i * 64, 64), 64)
            grad, one = back[at, :], unit[at, :]
            gains = gains + jnp.sum((grad * one).reshape(8, 8, chans), axis=0)
            scaled = grad * gain[...]
            mean = jnp.mean(scaled, axis=-1, keepdims=True)
            along = jnp.mean(scaled * one, axis=-1, keepdims=True)
            d_filt[at, :] = inv[at, 0:1] * (scaled - mean - one * along)
            slot = i * lines // rows
            line = pl.ds(i * lines - slot * rows, lines)
            value = branch[at, :]
            held = cotan[slot, line].reshape(64, chans).astype(f32)
            scales = scales + jnp.sum((held * value).reshape(8, 8, chans), axis=0)
            cells = tiles[slot, line].reshape(64, chans).astype(f32)
            filled = (cells + scale[...] * value).astype(bf16)
            out[slot, line] = filled.reshape(lines, cols, chans)
            return gains, scales

        start = jnp.zeros((8, chans), f32)
        gain_grad[...], scale_grad[...] = lax.fori_loop(0, pixels // 64, finish, (start, start))
        for slot in range(WORK):
            begin, end = slot * rows * cols, (slot + 1) * rows * cols
            ends = (REACH, cols, chans)
            d_head[slot] = d_filt[begin : begin + REACH * cols, :].reshape(ends).astype(bf16)
            d_tail[slot] = d_filt[end - REACH * cols : end, :].reshape(ends).astype(bf16)


def tap_kernel(tiles, above, below, d_filt, gains, scales, small, pad, total, lines):
    slot = pl.program_id(0)
    rows, cols, chans = tiles.shape[1:]
    share = -(-(TAPS * TAPS + 2) // small.shape[0])

    @pl.when(slot == 0)
    def _():
        clear_padded(pad)
        total[...] = jnp.zeros_like(total)

    def line_of(r, lanes):
        return tiles[0, r, :, lanes]

    fill_padded(pad, above, line_of, below, rows, cols, chans)

    def over(i, lanes):
        for half in range(cols // 8):
            back = [d_filt[pl.ds(p * cols + 8 * half, 8), lanes] for p in range(rows)]
            for b in range(TAPS):
                line = window(pad, i, half, b, rows)
                for a in range(TAPS):
                    m = [line[p + a] * back[p] for p in range(rows)]
                    while len(m) > 1:
                        m = [m[p] + m[p + 1] for p in range(0, len(m), 2)]
                    total[a * TAPS + b, :, lanes] += m[0]

    lane_blocks(chans, over)

    @pl.when(slot == pl.num_programs(0) - 1)
    def _():
        lines[...] = jnp.zeros_like(lines)
        for i in range(TAPS * TAPS + 2):
            value = total[i] if i < TAPS * TAPS else (gains, scales)[i - TAPS * TAPS][...]
            at = i // share * small.shape[1] + i % share
            lines[at : at + 1, :] = jnp.sum(value, axis=0, keepdims=True)
        for i in range(small.shape[0]):
            small[i] = lines[i * small.shape[1] : (i + 1) * small.shape[1], :].astype(bf16)


def input_kernel(d_filt, above, below, cotan, kernel, out, sent, pad, wide):
    rows, cols, chans = out.shape[1:]

    @pl.when(pl.program_id(0) == 0)
    def _():
        spread_kernel(wide, kernel)
        clear_padded(pad)

    def line_of(r, lanes):
        return d_filt[pl.ds(r * cols, cols), lanes]

    fill_padded(pad, above, line_of, below, rows, cols, chans)

    def emit(p, half, lanes, value):
        at = pl.ds(8 * half, 8)
        out[0, p, at, lanes] = value + cotan[0, p, at, lanes].astype(f32)

    stencil(pad, wide, rows, cols, chans, True, emit)
    sent[...] = out[...].astype(bf16)


def to_partner(cells):
    slides = lax.axis_size("slide")
    return lax.ppermute(cells, "slide", [(i, (i + slides // 2) % slides) for i in range(slides)])


def all_slots(done, returned, count, slots):
    first, second = done[0], done[1]
    third = returned.astype(done.dtype)
    none = jnp.zeros_like(first)
    kept = [first, jnp.where(count >= 2, second, none), jnp.where(count >= 3, third, none)]
    return jnp.stack(kept + [none] * (slots - len(kept)))[None]


def body(tiles, cotangent, tile_counts, dw_kernel, ln_gain, fc1_weight, fc2_weight, layer_scale):
    _, slots, rows, cols, chans = tiles.shape
    hidden = fc1_weight.shape[0]
    pixels = rows * cols
    every = WORK * pixels
    count = tile_counts[0]
    lone = tiles[0, :1]
    above0, below0 = edges(lone[:, :REACH], lone[:, rows - REACH :])
    moved = to_partner(tiles[0, 2]), to_partner(cotangent[0, 2])
    second_tile, second_cotan = (
        jnp.where(count >= 2, own[0, 1], came)[None]
        for own, came in zip((tiles, cotangent), moved, strict=True)
    )
    above1, below1 = edges(second_tile[:, :REACH], second_tile[:, rows - REACH :])
    taps = dw_kernel.reshape(TAPS * TAPS, chans)
    gain, scale = ln_gain[None], layer_scale[None]

    params = pltpu.CompilerParams(
        vmem_limit_bytes=60 * 1024 * 1024, dimension_semantics=("arbitrary",)
    )
    shape = jax.ShapeDtypeStruct
    brief = pl.CostEstimate(flops=1, bytes_accessed=1, transcendentals=0)
    smem = pl.BlockSpec(memory_space=pltpu.SMEM)
    tile = pl.BlockSpec((1, rows, cols, chans), lambda s: (s, 0, 0, 0))
    edge = pl.BlockSpec((1, REACH, cols, chans), lambda s: (s, 0, 0, 0))
    flat = pl.BlockSpec((pixels, chans), lambda s: (s, 0))

    def whole(*dims):
        return pl.BlockSpec(dims, lambda s: (0,) * len(dims))

    pad = pltpu.VMEM((chans // LANES, (rows + 2 * REACH) * PITCH + 8, LANES), f32)
    wide = pltpu.VMEM((TAPS * TAPS, 8, chans), f32)

    def forward(at, tile_in, above, below, cotan, earlier):
        one = pl.BlockSpec((1, rows, cols, chans), lambda s: (0, 0, 0, 0))
        line = pl.BlockSpec((1, REACH, cols, chans), lambda s: (0, 0, 0, 0))
        block = pl.BlockSpec((pixels, chans), lambda s: (at, 0))
        return pl.pallas_call(
            forward_kernel,
            grid=(1,),
            in_specs=[one, line, line, one, whole(TAPS * TAPS, chans), whole(1, chans), whole(1, chans)]
            + [pl.BlockSpec(memory_space=pl.ANY)] * len(earlier),
            out_specs=[block, block, pl.BlockSpec((pixels, LANES), lambda s: (at, 0)), block],
            out_shape=[
                shape((every, chans), bf16),
                shape((every, chans), f32),
                shape((every, LANES), f32),
                shape((every, chans), bf16),
            ],
            scratch_shapes=[pad, wide, pltpu.VMEM((pixels, chans), f32)],
            input_output_aliases={7 + i: i for i in range(len(earlier))},
            compiler_params=params,
            cost_estimate=brief,
            name="forward",
        )(tile_in, above, below, cotan, taps, gain, scale, *earlier)

    earlier = forward(0, lone, above0, below0, cotangent[0, :1], [])
    normed, unit, inv, spread = forward(1, second_tile, above1, below1, second_cotan, earlier)
    above, below = jnp.concatenate([above0, above1]), jnp.concatenate([below0, below1])
    cotangent = jnp.concatenate([cotangent[0, :1], second_cotan])
    tiles = jnp.concatenate([lone, second_tile])

    chips = SIDE * SIDE
    halves = shape((SIDE, SIDE, SIDE, hidden // (8 * chips), chans), bf16)
    d_edge = shape((WORK, REACH, cols, chans), bf16)
    core = (lax.axis_index("slide") % 2).reshape(1)

    def once(*dims):
        return pl.BlockSpec(dims, lambda s: (0,) * len(dims), pipeline_mode=pl.Buffered(1))

    quarter_of = pl.BlockSpec((SIDE, 1, *halves.shape[2:]), lambda j: (0, j, 0, 0, 0))
    live = once(*tiles.shape)
    mine1, other1, mine2, other2, d_filt, d_head, d_tail, block_out, gain_grad, scale_grad = pl.pallas_call(
        mlp_kernel,
        grid=(hidden // BLOCK,),
        in_specs=[
            smem,
            once(every, chans),
            once(every, chans),
            pl.BlockSpec((BLOCK, chans), lambda j: (j, 0)),
            pl.BlockSpec((chans, BLOCK), lambda j: (0, j)),
            once(every, chans),
            once(every, LANES),
            once(1, chans),
            once(1, chans),
            live,
            live,
        ],
        out_specs=[
            quarter_of,
            quarter_of,
            once(*halves.shape),
            once(*halves.shape),
            once(every, chans),
            once(*d_edge.shape),
            once(*d_edge.shape),
            once(*tiles.shape),
            once(8, chans),
            once(8, chans),
        ],
        out_shape=[
            halves,
            halves,
            halves,
            halves,
            shape((every, chans), f32),
            d_edge,
            d_edge,
            shape(tiles.shape, bf16),
            shape((8, chans), f32),
            shape((8, chans), f32),
        ],
        scratch_shapes=[
            pltpu.VMEM((chans, every), bf16),
            pltpu.VMEM((chans // LANES, hidden, LANES), f32),
            pltpu.VMEM((BLOCK, chans), f32),
            pltpu.VMEM((every, chans), f32),
            pltpu.VMEM((every, chans), f32),
        ],
        compiler_params=params,
        cost_estimate=brief,
        name="mlp",
    )(
        core, normed, spread, fc1_weight, fc2_weight, unit, inv, gain, scale, tiles, cotangent
    )

    got2, got1 = from_other_core(other2), from_other_core(other1)
    d_above, d_below = edges(d_head, d_tail)

    lines = -(-(TAPS * TAPS + 2) // chips)
    small = shape((chips, -(-lines // 8) * 8, chans), bf16)
    small = pl.pallas_call(
        tap_kernel,
        grid=(WORK,),
        in_specs=[tile, edge, edge, flat, whole(8, chans), whole(8, chans)],
        out_specs=whole(*small.shape),
        out_shape=small,
        scratch_shapes=[pad, wide, pltpu.VMEM((chips * small.shape[1], chans), f32)],
        compiler_params=params,
        cost_estimate=brief,
        name="taps",
    )(tiles, above, below, d_filt, gain_grad, scale_grad)

    small, d_above, d_below, mine1, got1, mine2, got2 = after(
        small, d_above, d_below, mine1, got1, mine2, got2
    )
    share = plane_exchanged(small)[:lines]
    parts = quarters(mine2, got2) + quarters(mine1, got1)
    ring2, ring1 = ring_sent(parts[:SIDE]), ring_sent(parts[SIDE:])
    share, _, _ = after(share, parts[SIDE - 1], parts[-1])
    block_back = to_partner(block_out[1])
    share, d_filt, d_above, d_below, block_back = after(share, d_filt, d_above, d_below, block_back)
    small = everywhere(share)

    grad_input, grad_sent = pl.pallas_call(
        input_kernel,
        grid=(WORK,),
        in_specs=[flat, edge, edge, tile, whole(TAPS * TAPS, chans)],
        out_specs=[tile, whole(1, rows, cols, chans)],
        out_shape=[shape(tiles.shape, f32), shape((1, rows, cols, chans), bf16)],
        scratch_shapes=[pad, wide],
        compiler_params=params,
        cost_estimate=brief,
        name="inputs",
    )(d_filt, d_above, d_below, cotangent, taps)

    grad_kernel = small[: TAPS * TAPS].reshape(dw_kernel.shape)
    blocks = jnp.concatenate([total_of(parts[0], ring2), total_of(parts[SIDE], ring1)], axis=1)
    blocks, small, grad_input, grad_sent = after(blocks, small, grad_input, grad_sent)
    grad_back = to_partner(grad_sent[0])
    block_out = all_slots(block_out, block_back, count, slots)
    grad_input = all_slots(grad_input, grad_back, count, slots)
    sums = plane_exchanged(blocks)
    own = hidden // (8 * chips)
    grad_fc2 = sums[:own].reshape(-1, hidden)
    grad_fc1 = sums[own:]
    return (
        block_out,
        grad_input,
        grad_fc1,
        grad_fc2,
        grad_kernel,
        small[TAPS * TAPS],
        small[TAPS * TAPS + 1],
    )


def solution(mesh):
    in_specs = (
        P("slide", None, "row", None, None),
        P("slide", None, "row", None, None),
        P("slide"),
        P(),
        P(),
        P(),
        P(),
        P(),
    )
    out_specs = (
        P("slide", None, "row", None, None),
        P("slide", None, "row", None, None),
        P(("slide", "row"), None),
        P(("slide", "row"), None),
        P(),
        P(),
        P(),
    )
    return jax.shard_map(body, mesh=mesh, in_specs=in_specs, out_specs=out_specs, check_vma=False)
```

```python
import functools
import itertools
import math

import jax
import jax.numpy as jnp
from jax import lax
from jax.experimental import pallas as pl
from jax.experimental.pallas import tpu as pltpu
from jax.sharding import PartitionSpec as P

epsilon = 1e-06
root_half = 1.0 / math.sqrt(2.0)
density = 1.0 / math.sqrt(2.0 * math.pi)
f32, bf16 = jnp.float32, jnp.bfloat16
REACH = 3
TAPS = 7
LEFT = 8
LANES = 128
MOST = 3
BLOCK = 768
SIDE = 4
PITCH = 24


def place(y, x, core, z):
    return ((y * SIDE + x) * 2 + core) * SIDE + z


def after(*values):
    return lax.optimization_barrier(values)


def from_other_core(half):
    return lax.ppermute(half, "slide", [(i, i ^ 1) for i in range(lax.axis_size("slide"))])


def quarters(mine, got):
    core = lax.axis_index("slide") % 2
    own = jnp.where(core == 0, lax.axis_index("row"), lax.axis_index("slide") // 2 % SIDE)

    def cut(half, by):
        return lax.dynamic_index_in_dim(half, (own + by) % SIDE, 0, keepdims=False).astype(f32)

    return [(cut(mine, by) + cut(got, by)).astype(bf16) for by in range(SIDE)]


def ring_sent(parts):
    every = [range(SIDE)] * 3
    pairs = [
        [
            move
            for y, x, z in itertools.product(*every)
            for move in (
                (place(y, x, 0, z), place(y, x, 0, (z + by) % SIDE)),
                (place(y, x, 1, z), place(y, (x + by) % SIDE, 1, z)),
            )
        ]
        for by in range(SIDE)
    ]
    return [lax.ppermute(parts[by], ("slide", "row"), pairs[by]) for by in range(1, SIDE)]


def total_of(own, got):
    total = own.astype(f32)
    for part in got:
        total = total + part.astype(f32)
    return total.astype(bf16).reshape(SIDE * SIDE, -1, own.shape[-1])


def plane_exchanged(blocks):
    every = [range(SIDE)] * 2
    groups = [[place(y, x, 0, z) for y, x in itertools.product(*every)] for z in range(SIDE)]
    groups += [[place(y, x, 1, z) for y, z in itertools.product(*every)] for x in range(SIDE)]
    got = lax.all_to_all(
        blocks.reshape(-1, blocks.shape[-1]),
        ("slide", "row"),
        0,
        0,
        axis_index_groups=groups,
        tiled=True,
    )
    return jnp.sum(got.reshape(blocks.shape).astype(f32), axis=0)


def everywhere(share):
    count = lax.axis_size("slide") * lax.axis_size("row")
    cells = share.astype(bf16).reshape(-1, LANES)
    sent = jnp.broadcast_to(cells[None], (count, *cells.shape))
    got = lax.all_to_all(sent, ("slide", "row"), 0, 0, tiled=True)
    got = got.reshape(SIDE, SIDE, 2, SIDE, *cells.shape).astype(f32)
    whole = jnp.sum(got[:, :, 0], axis=2) + jnp.sum(got[:, :, 1], axis=1)
    return whole.reshape(-1, share.shape[-1])


def edges(head, tail):
    ends = lax.axis_size("row") - 1
    above = lax.ppermute(tail, "row", [(i, i + 1) for i in range(ends)])
    below = lax.ppermute(head, "row", [(i + 1, i) for i in range(ends)])
    return above, below


def clear_padded(pad):
    pad[...] = jnp.zeros_like(pad)


def lane_blocks(chans, body):
    def step(i, carry):
        body(i, pl.ds(pl.multiple_of(i * LANES, LANES), LANES))
        return carry

    lax.fori_loop(0, chans // LANES, step, 0)


def fill_padded(pad, above, line_of, below, rows, cols, chans):
    def over(i, lanes):
        for r in range(REACH):
            pad[i, pl.ds(r * PITCH + LEFT, cols), :] = above[0, r, :, lanes].astype(f32)
            at = (rows + REACH + r) * PITCH + LEFT
            pad[i, pl.ds(at, cols), :] = below[0, r, :, lanes].astype(f32)
        for r in range(rows):
            pad[i, pl.ds((REACH + r) * PITCH + LEFT, cols), :] = line_of(r, lanes).astype(f32)

    lane_blocks(chans, over)


def window(pad, i, half, b, rows):
    shift = LEFT - REACH + b + 8 * half
    return [pad[i, pl.ds(r * PITCH + shift, 8), :] for r in range(rows + 2 * REACH)]


def stencil(pad, wide, rows, cols, chans, flip, emit):
    def over(i, lanes):
        for half in range(cols // 8):
            total = [None] * rows
            for b in range(TAPS):
                line = window(pad, i, half, b, rows)
                weights = []
                for a in range(TAPS):
                    tap = a * TAPS + b
                    weights.append(wide[TAPS * TAPS - 1 - tap if flip else tap, :, lanes])
                for p in range(rows):
                    m = [weights[a] * line[p + a] for a in range(TAPS)]
                    part = ((m[0] + m[1]) + (m[2] + m[3])) + ((m[4] + m[5]) + m[6])
                    total[p] = part if total[p] is None else total[p] + part
            for p in range(rows):
                emit(p, half, lanes, total[p])

    lane_blocks(chans, over)


def spread_kernel(wide, kernel_ref):
    for tap in range(TAPS * TAPS):
        a, b = divmod(tap, TAPS)
        wide[tap] = jnp.broadcast_to(kernel_ref[a, b : b + 1, :], wide.shape[1:])


def forward_kernel(
    count, tiles, above, below, cotan, kernel, gain, scale, normed, unit, spread, held_out, pad, wide, filt
):
    slot = pl.program_id(0)
    rows, cols, chans = tiles.shape[2:]

    @pl.when(slot == 0)
    def _():
        spread_kernel(wide, kernel)
        clear_padded(pad)

    def line_of(r, lanes):
        return tiles[0, 0, r, :, lanes]

    fill_padded(pad, above, line_of, below, rows, cols, chans)

    def emit(p, half, lanes, value):
        filt[pl.ds(p * cols + 8 * half, 8), lanes] = value

    stencil(pad, wide, rows, cols, chans, False, emit)
    weight = (slot < count[0]).astype(f32)
    held = cotan[...].reshape(rows * cols, chans).astype(f32) * weight
    held_out[...] = (held * scale[...]).astype(bf16)

    def norm(i, carry):
        at = pl.ds(pl.multiple_of(i * 64, 64), 64)
        value = filt[at, :]
        center = value - jnp.mean(value, axis=-1, keepdims=True)
        inv_std = lax.rsqrt(jnp.mean(center * center, axis=-1, keepdims=True) + epsilon)
        one = center * inv_std
        unit[at, :] = one
        normed[at, :] = (one * gain[...]).astype(bf16)
        spread[at, :] = jnp.broadcast_to(inv_std, (64, LANES))
        return carry

    lax.fori_loop(0, rows * cols // 64, norm, 0)


def gelu_parts(pre):
    size = jnp.abs(pre)
    bell = jnp.exp(pre * pre * -0.5)
    t = 1.0 / (1.0 + (0.3275911 * root_half) * size)
    poly = t * (
        0.5 * 0.254829592
        + t * (0.5 * -0.284496736 + t * (0.5 * 1.421413741 + t * (0.5 * -1.453152027 + t * (0.5 * 1.061405429))))
    )
    tail = poly * bell
    return jnp.where(pre < 0.0, tail, 1.0 - tail), bell * density


def split_rows(core, mine, other, y, first, rows_at):
    count = mine.shape[3]
    for x, z in itertools.product(range(SIDE), repeat=2):
        flipped = [jnp.where(core[0] == 0, *pair) for pair in ((z, x), (x, z))]
        for half, which, at in ((mine, core[0], flipped), (other, 1 - core[0], flipped[::-1])):
            begin = pl.multiple_of(first + ((2 * x + which) * SIDE + z) * count, 8)
            rows_at(half, (at[0], y, at[1]), pl.ds(begin, count))


def mlp_kernel(
    core, count, normed, spread, first, second, unit, inv, gain, scale, tiles, cotan,
    mine1, other1, mine2, other2, d_filt, d_head, d_tail, out, gain_grad, scale_grad,
    turned, total2, term, back, branch,
):
    step = pl.program_id(0)
    pixels, chans = normed.shape
    rows, cols = tiles.shape[2:4]

    @pl.when(step == 0)
    def _():
        turned[...] = spread[...].T
        back[...] = jnp.zeros_like(back)
        branch[...] = jnp.zeros_like(branch)

    pre = lax.dot_general(
        normed[...], first[...], (((1,), (1,)), ((), ())), preferred_element_type=f32
    )
    d_act = jnp.dot(spread[...], second[...], preferred_element_type=f32)
    cdf, pdf = gelu_parts(pre)
    active = (pre * cdf).astype(bf16)
    d_pre = (d_act * (cdf + pre * pdf)).astype(bf16)
    grad = jnp.dot(turned[...], active, preferred_element_type=f32)
    for i in range(BLOCK // LANES):
        total2[i, pl.ds(step, chans, stride=4), :] = grad[:, i * LANES : (i + 1) * LANES]
    branch[...] += lax.dot_general(
        active, second[...], (((1,), (1,)), ((), ())), preferred_element_type=f32
    )
    term[...] = lax.dot_general(
        d_pre, normed[...], (((0,), (0,)), ((), ())), preferred_element_type=f32
    )

    def copy1(half, chip, at):
        half[chip] = term[at, :].astype(bf16)

    split_rows(core, mine1, other1, 0, 0, copy1)
    back[...] += jnp.dot(d_pre, first[...], preferred_element_type=f32)

    @pl.when(step == pl.num_programs(0) - 1)
    def _():
        def copy2(half, chip, at):
            for i in range(BLOCK // LANES):
                lanes = slice(i * LANES, (i + 1) * LANES)
                half[(*chip, slice(None), lanes)] = total2[i, at, :].astype(bf16)

        def over(y, carry):
            split_rows(core, mine2, other2, y, y * (total2.shape[1] // SIDE), copy2)
            return carry

        lax.fori_loop(0, SIDE, over, 0)
        lines = 64 // cols

        def finish(i, kept):
            gains, scales = kept
            at = pl.ds(pl.multiple_of(i * 64, 64), 64)
            grad, one = back[at, :], unit[at, :]
            gains = gains + jnp.sum((grad * one).reshape(8, 8, chans), axis=0)
            scaled = grad * gain[...]
            mean = jnp.mean(scaled, axis=-1, keepdims=True)
            along = jnp.mean(scaled * one, axis=-1, keepdims=True)
            d_filt[at, :] = inv[at, 0:1] * (scaled - mean - one * along)
            slot = i * lines // rows
            weight = (slot < count[0]).astype(f32)
            line = pl.ds(i * lines - slot * rows, lines)
            value = branch[at, :]
            held = cotan[0, slot, line].reshape(64, chans).astype(f32) * weight
            scales = scales + jnp.sum((held * value).reshape(8, 8, chans), axis=0)
            cells = tiles[0, slot, line].reshape(64, chans).astype(f32)
            filled = ((cells + scale[...] * value) * weight).astype(bf16)
            out[0, slot, line] = filled.reshape(lines, cols, chans)
            return gains, scales

        start = jnp.zeros((8, chans), f32)
        gain_grad[...], scale_grad[...] = lax.fori_loop(0, pixels // 64, finish, (start, start))
        for slot in range(MOST):
            begin, end = slot * rows * cols, (slot + 1) * rows * cols
            ends = (REACH, cols, chans)
            d_head[slot] = d_filt[begin : begin + REACH * cols, :].reshape(ends).astype(bf16)
            d_tail[slot] = d_filt[end - REACH * cols : end, :].reshape(ends).astype(bf16)
        out[0, MOST:] = jnp.zeros((out.shape[1] - MOST, rows, cols, chans), bf16)


def tap_kernel(tiles, above, below, d_filt, gains, scales, small, pad, total, lines):
    slot = pl.program_id(0)
    rows, cols, chans = tiles.shape[2:]
    share = -(-(TAPS * TAPS + 2) // small.shape[0])

    @pl.when(slot == 0)
    def _():
        clear_padded(pad)
        total[...] = jnp.zeros_like(total)

    def line_of(r, lanes):
        return tiles[0, 0, r, :, lanes]

    fill_padded(pad, above, line_of, below, rows, cols, chans)

    def over(i, lanes):
        for half in range(cols // 8):
            back = [d_filt[pl.ds(p * cols + 8 * half, 8), lanes] for p in range(rows)]
            for b in range(TAPS):
                line = window(pad, i, half, b, rows)
                for a in range(TAPS):
                    m = [line[p + a] * back[p] for p in range(rows)]
                    while len(m) > 1:
                        m = [m[p] + m[p + 1] for p in range(0, len(m), 2)]
                    total[a * TAPS + b, :, lanes] += m[0]

    lane_blocks(chans, over)

    @pl.when(slot == pl.num_programs(0) - 1)
    def _():
        lines[...] = jnp.zeros_like(lines)
        for i in range(TAPS * TAPS + 2):
            value = total[i] if i < TAPS * TAPS else (gains, scales)[i - TAPS * TAPS][...]
            at = i // share * small.shape[1] + i % share
            lines[at : at + 1, :] = jnp.sum(value, axis=0, keepdims=True)
        for i in range(small.shape[0]):
            small[i] = lines[i * small.shape[1] : (i + 1) * small.shape[1], :].astype(bf16)


def input_kernel(first, count, d_filt, above, below, cotan, kernel, *refs):
    out, pad, wide = refs[-3:]
    slot = pl.program_id(0) + first
    rows, cols, chans = out.shape[2:]

    @pl.when(slot == first)
    def _():
        spread_kernel(wide, kernel)
        clear_padded(pad)

    @pl.when(slot < MOST)
    def _():
        def line_of(r, lanes):
            return d_filt[pl.ds(r * cols, cols), lanes]

        fill_padded(pad, above, line_of, below, rows, cols, chans)
        weight = (slot < count[0]).astype(f32)

        def emit(p, half, lanes, value):
            at = pl.ds(8 * half, 8)
            out[0, 0, p, at, lanes] = value + cotan[0, 0, p, at, lanes].astype(f32) * weight

        stencil(pad, wide, rows, cols, chans, True, emit)

    @pl.when(slot >= MOST)
    def _():
        out[...] = jnp.zeros_like(out)


def body(tiles, cotangent, tile_counts, dw_kernel, ln_gain, fc1_weight, fc2_weight, layer_scale):
    _, slots, rows, cols, chans = tiles.shape
    hidden = fc1_weight.shape[0]
    pixels = rows * cols
    every = MOST * pixels
    gain, scale = ln_gain[None], layer_scale[None]
    above, below = edges(tiles[0, :MOST, :REACH], tiles[0, :MOST, rows - REACH :])

    params = pltpu.CompilerParams(
        vmem_limit_bytes=60 * 1024 * 1024, dimension_semantics=("arbitrary",)
    )
    shape = jax.ShapeDtypeStruct
    brief = pl.CostEstimate(flops=1, bytes_accessed=1, transcendentals=0)
    smem = pl.BlockSpec(memory_space=pltpu.SMEM)
    tile = pl.BlockSpec((1, 1, rows, cols, chans), lambda s: (0, s, 0, 0, 0))
    edge = pl.BlockSpec((1, REACH, cols, chans), lambda s: (s, 0, 0, 0))
    flat = pl.BlockSpec((pixels, chans), lambda s: (s, 0))

    def whole(*dims):
        return pl.BlockSpec(dims, lambda s: (0,) * len(dims))

    pad = pltpu.VMEM((chans // LANES, (rows + 2 * REACH) * PITCH + 8, LANES), f32)
    wide = pltpu.VMEM((TAPS * TAPS, 8, chans), f32)

    normed, unit, inv, spread = pl.pallas_call(
        forward_kernel,
        grid=(MOST,),
        in_specs=[smem, tile, edge, edge, tile, whole(TAPS, TAPS, chans), whole(1, chans), whole(1, chans)],
        out_specs=[flat, flat, pl.BlockSpec((pixels, LANES), lambda s: (s, 0)), flat],
        out_shape=[
            shape((every, chans), bf16),
            shape((every, chans), f32),
            shape((every, LANES), f32),
            shape((every, chans), bf16),
        ],
        scratch_shapes=[pad, wide, pltpu.VMEM((pixels, chans), f32)],
        compiler_params=params,
        cost_estimate=brief,
        name="forward",
    )(tile_counts, tiles, above, below, cotangent, dw_kernel, gain, scale)

    chips = SIDE * SIDE
    halves = shape((SIDE, SIDE, SIDE, hidden // (8 * chips), chans), bf16)
    d_edge = shape((MOST, REACH, cols, chans), bf16)
    core = (lax.axis_index("slide") % 2).reshape(1)

    def once(*dims):
        return pl.BlockSpec(dims, lambda s: (0,) * len(dims), pipeline_mode=pl.Buffered(1))

    quarter_of = pl.BlockSpec((SIDE, 1, *halves.shape[2:]), lambda j: (0, j, 0, 0, 0))
    live = once(1, MOST, rows, cols, chans)
    mine1, other1, mine2, other2, d_filt, d_head, d_tail, block_out, gain_grad, scale_grad = pl.pallas_call(
        mlp_kernel,
        grid=(hidden // BLOCK,),
        in_specs=[
            smem,
            smem,
            once(every, chans),
            once(every, chans),
            pl.BlockSpec((BLOCK, chans), lambda j: (j, 0)),
            pl.BlockSpec((chans, BLOCK), lambda j: (0, j)),
            once(every, chans),
            once(every, LANES),
            once(1, chans),
            once(1, chans),
            live,
            live,
        ],
        out_specs=[
            quarter_of,
            quarter_of,
            once(*halves.shape),
            once(*halves.shape),
            once(every, chans),
            once(*d_edge.shape),
            once(*d_edge.shape),
            once(*tiles.shape),
            once(8, chans),
            once(8, chans),
        ],
        out_shape=[
            halves,
            halves,
            halves,
            halves,
            shape((every, chans), f32),
            d_edge,
            d_edge,
            shape(tiles.shape, bf16),
            shape((8, chans), f32),
            shape((8, chans), f32),
        ],
        scratch_shapes=[
            pltpu.VMEM((chans, every), bf16),
            pltpu.VMEM((chans // LANES, hidden, LANES), f32),
            pltpu.VMEM((BLOCK, chans), f32),
            pltpu.VMEM((every, chans), f32),
            pltpu.VMEM((every, chans), f32),
        ],
        compiler_params=params,
        cost_estimate=brief,
        name="mlp",
    )(
        core, tile_counts, normed, spread, fc1_weight, fc2_weight, unit, inv, gain, scale, tiles, cotangent
    )

    got2, got1 = from_other_core(other2), from_other_core(other1)
    d_above, d_below = edges(d_head, d_tail)

    lines = -(-(TAPS * TAPS + 2) // chips)
    small = shape((chips, -(-lines // 8) * 8, chans), bf16)
    small = pl.pallas_call(
        tap_kernel,
        grid=(MOST,),
        in_specs=[tile, edge, edge, flat, whole(8, chans), whole(8, chans)],
        out_specs=whole(*small.shape),
        out_shape=small,
        scratch_shapes=[pad, wide, pltpu.VMEM((chips * small.shape[1], chans), f32)],
        compiler_params=params,
        cost_estimate=brief,
        name="taps",
    )(tiles, above, below, d_filt, gain_grad, scale_grad)

    small, d_above, d_below, mine1, got1, mine2, got2 = after(
        small, d_above, d_below, mine1, got1, mine2, got2
    )
    share = plane_exchanged(small)[:lines]
    parts2, parts1 = quarters(mine2, got2), quarters(mine1, got1)
    ring2, ring1 = ring_sent(parts2), ring_sent(parts1)
    share, _, _ = after(share, parts2[-1], parts1[-1])
    share, d_filt, d_above, d_below = after(share, d_filt, d_above, d_below)
    small = everywhere(share)

    def input_grads(first, some, earlier, d_filt, d_above, d_below):
        def at(s):
            return jnp.minimum(s + first, MOST - 1)

        tile_at = (1, 1, rows, cols, chans)
        edge_at = pl.BlockSpec((1, REACH, cols, chans), lambda s: (at(s), 0, 0, 0))
        return pl.pallas_call(
            functools.partial(input_kernel, first),
            grid=(some,),
            in_specs=[
                smem,
                pl.BlockSpec((pixels, chans), lambda s: (at(s), 0)),
                edge_at,
                edge_at,
                pl.BlockSpec(tile_at, lambda s: (0, at(s), 0, 0, 0)),
                whole(TAPS, TAPS, chans),
            ]
            + [pl.BlockSpec(memory_space=pl.ANY)] * len(earlier),
            out_specs=pl.BlockSpec(tile_at, lambda s: (0, s + first, 0, 0, 0)),
            out_shape=shape(tiles.shape, f32),
            scratch_shapes=[pad, wide],
            input_output_aliases={6: 0} if earlier else {},
            compiler_params=params,
            cost_estimate=brief,
            name="inputs",
        )(tile_counts, d_filt, d_above, d_below, cotangent, dw_kernel, *earlier)

    grad_input = input_grads(0, 2, [], d_filt, d_above, d_below)

    grad_kernel = small[: TAPS * TAPS].reshape(dw_kernel.shape)
    blocks = jnp.concatenate([total_of(parts2[0], ring2), total_of(parts1[0], ring1)], axis=1)
    blocks, small, grad_input, d_filt = after(blocks, small, grad_input, d_filt)
    grad_input = input_grads(2, slots - 2, [grad_input], d_filt, d_above, d_below)
    sums = plane_exchanged(blocks)
    own = hidden // (8 * chips)
    grad_fc2 = sums[:own].reshape(-1, hidden)
    grad_fc1 = sums[own:]
    return (
        block_out,
        grad_input,
        grad_fc1,
        grad_fc2,
        grad_kernel,
        small[TAPS * TAPS],
        small[TAPS * TAPS + 1],
    )


def solution(mesh):
    in_specs = (
        P("slide", None, "row", None, None),
        P("slide", None, "row", None, None),
        P("slide"),
        P(),
        P(),
        P(),
        P(),
        P(),
    )
    out_specs = (
        P("slide", None, "row", None, None),
        P("slide", None, "row", None, None),
        P(("slide", "row"), None),
        P(("slide", "row"), None),
        P(),
        P(),
        P(),
    )
    return jax.shard_map(body, mesh=mesh, in_specs=in_specs, out_specs=out_specs, check_vma=False)
```

```python
import functools
import itertools
import math

import jax
import jax.numpy as jnp
from jax import lax
from jax.experimental import pallas as pl
from jax.experimental.pallas import tpu as pltpu
from jax.sharding import PartitionSpec as P

epsilon = 1e-06
root_half = 1.0 / math.sqrt(2.0)
density = 1.0 / math.sqrt(2.0 * math.pi)
f32, bf16 = jnp.float32, jnp.bfloat16
REACH = 3
TAPS = 7
LEFT = 8
LANES = 128
MOST = 3
BLOCK = 768
SIDE = 4
PITCH = 24


def place(y, x, core, z):
    return ((y * SIDE + x) * 2 + core) * SIDE + z


def after(*values):
    return lax.optimization_barrier(values)


def from_other_core(half):
    return lax.ppermute(half, "slide", [(i, i ^ 1) for i in range(lax.axis_size("slide"))])


def quarters(mine, got):
    core = lax.axis_index("slide") % 2
    own = jnp.where(core == 0, lax.axis_index("row"), lax.axis_index("slide") // 2 % SIDE)

    def cut(half, by):
        return lax.dynamic_index_in_dim(half, (own + by) % SIDE, 0, keepdims=False).astype(f32)

    return [(cut(mine, by) + cut(got, by)).astype(bf16) for by in range(SIDE)]


def ring_sent(parts):
    every = [range(SIDE)] * 3
    pairs = [
        [
            move
            for y, x, z in itertools.product(*every)
            for move in (
                (place(y, x, 0, z), place(y, x, 0, (z + by) % SIDE)),
                (place(y, x, 1, z), place(y, (x + by) % SIDE, 1, z)),
            )
        ]
        for by in range(SIDE)
    ]
    return [lax.ppermute(parts[by], ("slide", "row"), pairs[by]) for by in range(1, SIDE)]


def total_of(own, got):
    total = own.astype(f32)
    for part in got:
        total = total + part.astype(f32)
    return total.astype(bf16).reshape(SIDE * SIDE, -1, own.shape[-1])


def plane_exchanged(blocks):
    every = [range(SIDE)] * 2
    groups = [[place(y, x, 0, z) for y, x in itertools.product(*every)] for z in range(SIDE)]
    groups += [[place(y, x, 1, z) for y, z in itertools.product(*every)] for x in range(SIDE)]
    got = lax.all_to_all(
        blocks.reshape(-1, blocks.shape[-1]),
        ("slide", "row"),
        0,
        0,
        axis_index_groups=groups,
        tiled=True,
    )
    return jnp.sum(got.reshape(blocks.shape).astype(f32), axis=0)


def everywhere(share):
    count = lax.axis_size("slide") * lax.axis_size("row")
    cells = share.astype(bf16).reshape(-1, LANES)
    sent = jnp.broadcast_to(cells[None], (count, *cells.shape))
    got = lax.all_to_all(sent, ("slide", "row"), 0, 0, tiled=True)
    got = got.reshape(SIDE, SIDE, 2, SIDE, *cells.shape).astype(f32)
    whole = jnp.sum(got[:, :, 0], axis=2) + jnp.sum(got[:, :, 1], axis=1)
    return whole.reshape(-1, share.shape[-1])


def edges(head, tail):
    ends = lax.axis_size("row") - 1
    above = lax.ppermute(tail, "row", [(i, i + 1) for i in range(ends)])
    below = lax.ppermute(head, "row", [(i + 1, i) for i in range(ends)])
    return above, below


def clear_padded(pad):
    pad[...] = jnp.zeros_like(pad)


def lane_blocks(chans, body):
    def step(i, carry):
        body(i, pl.ds(pl.multiple_of(i * LANES, LANES), LANES))
        return carry

    lax.fori_loop(0, chans // LANES, step, 0)


def fill_padded(pad, above, line_of, below, rows, cols, chans):
    def over(i, lanes):
        for r in range(REACH):
            pad[i, pl.ds(r * PITCH + LEFT, cols), :] = above[0, r, :, lanes].astype(f32)
            at = (rows + REACH + r) * PITCH + LEFT
            pad[i, pl.ds(at, cols), :] = below[0, r, :, lanes].astype(f32)
        for r in range(rows):
            pad[i, pl.ds((REACH + r) * PITCH + LEFT, cols), :] = line_of(r, lanes).astype(f32)

    lane_blocks(chans, over)


def window(pad, i, half, b, rows):
    shift = LEFT - REACH + b + 8 * half
    return [pad[i, pl.ds(r * PITCH + shift, 8), :] for r in range(rows + 2 * REACH)]


def stencil(pad, wide, rows, cols, chans, flip, emit):
    def over(i, lanes):
        for half in range(cols // 8):
            total = [None] * rows
            for b in range(TAPS):
                line = window(pad, i, half, b, rows)
                weights = []
                for a in range(TAPS):
                    tap = a * TAPS + b
                    weights.append(wide[TAPS * TAPS - 1 - tap if flip else tap, :, lanes])
                for p in range(rows):
                    m = [weights[a] * line[p + a] for a in range(TAPS)]
                    part = ((m[0] + m[1]) + (m[2] + m[3])) + ((m[4] + m[5]) + m[6])
                    total[p] = part if total[p] is None else total[p] + part
            for p in range(rows):
                emit(p, half, lanes, total[p])

    lane_blocks(chans, over)


def spread_kernel(wide, kernel_ref):
    for tap in range(TAPS * TAPS):
        a, b = divmod(tap, TAPS)
        wide[tap] = jnp.broadcast_to(kernel_ref[a, b : b + 1, :], wide.shape[1:])


def forward_step(
    slot, count, tiles, above, below, cotan, kernel, gain, scale, normed, unit, inv, spread, pad, wide, filt
):
    rows, cols, chans = tiles.shape[2:]
    base = slot * rows * cols

    @pl.when(slot == 0)
    def _():
        spread_kernel(wide, kernel)
        clear_padded(pad)

    def line_of(r, lanes):
        return tiles[0, slot, r, :, lanes]

    here = pl.ds(slot, 1)
    fill_padded(pad, above.at[here], line_of, below.at[here], rows, cols, chans)

    def emit(p, half, lanes, value):
        filt[pl.ds(p * cols + 8 * half, 8), lanes] = value

    stencil(pad, wide, rows, cols, chans, False, emit)
    weight = (slot < count[0]).astype(f32)
    held = cotan[0, slot].reshape(rows * cols, chans).astype(f32) * weight
    spread[pl.ds(pl.multiple_of(base, 256), rows * cols), :] = (held * scale[...]).astype(bf16)

    def norm(i, carry):
        at = pl.ds(pl.multiple_of(i * 64, 64), 64)
        value = filt[at, :]
        center = value - jnp.mean(value, axis=-1, keepdims=True)
        inv_std = lax.rsqrt(jnp.mean(center * center, axis=-1, keepdims=True) + epsilon)
        one = center * inv_std
        to = pl.ds(pl.multiple_of(base + i * 64, 64), 64)
        unit[to, :] = one
        normed[to, :] = (one * gain[...]).astype(bf16)
        inv[to, :] = jnp.broadcast_to(inv_std, (64, LANES))
        return carry

    lax.fori_loop(0, rows * cols // 64, norm, 0)


def gelu_parts(pre):
    size = jnp.abs(pre)
    bell = jnp.exp(pre * pre * -0.5)
    t = 1.0 / (1.0 + (0.3275911 * root_half) * size)
    poly = t * (
        0.5 * 0.254829592
        + t * (0.5 * -0.284496736 + t * (0.5 * 1.421413741 + t * (0.5 * -1.453152027 + t * (0.5 * 1.061405429))))
    )
    tail = poly * bell
    return jnp.where(pre < 0.0, tail, 1.0 - tail), bell * density


def split_rows(core, mine, other, y, first, rows_at):
    count = mine.shape[3]
    for x, z in itertools.product(range(SIDE), repeat=2):
        flipped = [jnp.where(core[0] == 0, *pair) for pair in ((z, x), (x, z))]
        for half, which, at in ((mine, core[0], flipped), (other, 1 - core[0], flipped[::-1])):
            begin = pl.multiple_of(first + ((2 * x + which) * SIDE + z) * count, 8)
            rows_at(half, (at[0], y, at[1]), pl.ds(begin, count))


def main_kernel(
    core, count, above, below, kernel, first, second, gain, scale, tiles, cotan,
    mine1, other1, mine2, other2, d_filt, d_head, d_tail, out, gain_grad, scale_grad,
    normed, spread, unit, inv, pad, wide, filt, *scratch,
):
    at = pl.program_id(0)

    @pl.when(at < MOST)
    def _():
        forward_step(
            at, count, tiles, above, below, cotan, kernel, gain, scale,
            normed, unit, inv, spread, pad, wide, filt,
        )

    @pl.when(at >= MOST)
    def _():
        mlp_step(
            at - MOST, core, count, normed, spread, first, second, unit, inv, gain, scale, tiles, cotan,
            mine1, other1, mine2, other2, d_filt, d_head, d_tail, out, gain_grad, scale_grad, *scratch,
        )


def mlp_step(
    step, core, count, normed, spread, first, second, unit, inv, gain, scale, tiles, cotan,
    mine1, other1, mine2, other2, d_filt, d_head, d_tail, out, gain_grad, scale_grad,
    turned, total2, term, back, branch,
):
    pixels, chans = normed.shape
    rows, cols = tiles.shape[2:4]

    @pl.when(step == 0)
    def _():
        turned[...] = spread[...].T
        back[...] = jnp.zeros_like(back)
        branch[...] = jnp.zeros_like(branch)

    pre = lax.dot_general(
        normed[...], first[...], (((1,), (1,)), ((), ())), preferred_element_type=f32
    )
    d_act = jnp.dot(spread[...], second[...], preferred_element_type=f32)
    cdf, pdf = gelu_parts(pre)
    active = (pre * cdf).astype(bf16)
    d_pre = (d_act * (cdf + pre * pdf)).astype(bf16)
    grad = jnp.dot(turned[...], active, preferred_element_type=f32)
    for i in range(BLOCK // LANES):
        total2[i, pl.ds(step, chans, stride=4), :] = grad[:, i * LANES : (i + 1) * LANES]
    branch[...] += lax.dot_general(
        active, second[...], (((1,), (1,)), ((), ())), preferred_element_type=f32
    )
    term[...] = lax.dot_general(
        d_pre, normed[...], (((0,), (0,)), ((), ())), preferred_element_type=f32
    )

    def copy1(half, chip, at):
        half[chip] = term[at, :].astype(bf16)

    split_rows(core, mine1, other1, 0, 0, copy1)
    back[...] += jnp.dot(d_pre, first[...], preferred_element_type=f32)

    @pl.when(step == total2.shape[1] // BLOCK - 1)
    def _():
        def copy2(half, chip, at):
            for i in range(BLOCK // LANES):
                lanes = slice(i * LANES, (i + 1) * LANES)
                half[(*chip, slice(None), lanes)] = total2[i, at, :].astype(bf16)

        def over(y, carry):
            split_rows(core, mine2, other2, y, y * (total2.shape[1] // SIDE), copy2)
            return carry

        lax.fori_loop(0, SIDE, over, 0)
        lines = 64 // cols

        def finish(i, kept):
            gains, scales = kept
            at = pl.ds(pl.multiple_of(i * 64, 64), 64)
            grad, one = back[at, :], unit[at, :]
            gains = gains + jnp.sum((grad * one).reshape(8, 8, chans), axis=0)
            scaled = grad * gain[...]
            mean = jnp.mean(scaled, axis=-1, keepdims=True)
            along = jnp.mean(scaled * one, axis=-1, keepdims=True)
            d_filt[at, :] = inv[at, 0:1] * (scaled - mean - one * along)
            slot = i * lines // rows
            weight = (slot < count[0]).astype(f32)
            line = pl.ds(i * lines - slot * rows, lines)
            value = branch[at, :]
            held = cotan[0, slot, line].reshape(64, chans).astype(f32) * weight
            scales = scales + jnp.sum((held * value).reshape(8, 8, chans), axis=0)
            cells = tiles[0, slot, line].reshape(64, chans).astype(f32)
            filled = ((cells + scale[...] * value) * weight).astype(bf16)
            out[0, slot, line] = filled.reshape(lines, cols, chans)
            return gains, scales

        start = jnp.zeros((8, chans), f32)
        gain_grad[...], scale_grad[...] = lax.fori_loop(0, pixels // 64, finish, (start, start))
        for slot in range(MOST):
            begin, end = slot * rows * cols, (slot + 1) * rows * cols
            ends = (REACH, cols, chans)
            d_head[slot] = d_filt[begin : begin + REACH * cols, :].reshape(ends).astype(bf16)
            d_tail[slot] = d_filt[end - REACH * cols : end, :].reshape(ends).astype(bf16)
        out[0, MOST:] = jnp.zeros((out.shape[1] - MOST, rows, cols, chans), bf16)


def tap_kernel(tiles, above, below, d_filt, gains, scales, small, pad, total, lines):
    slot = pl.program_id(0)
    rows, cols, chans = tiles.shape[2:]
    share = -(-(TAPS * TAPS + 2) // small.shape[0])

    @pl.when(slot == 0)
    def _():
        clear_padded(pad)
        total[...] = jnp.zeros_like(total)

    def line_of(r, lanes):
        return tiles[0, 0, r, :, lanes]

    fill_padded(pad, above, line_of, below, rows, cols, chans)

    def over(i, lanes):
        for half in range(cols // 8):
            back = [d_filt[pl.ds(p * cols + 8 * half, 8), lanes] for p in range(rows)]
            for b in range(TAPS):
                line = window(pad, i, half, b, rows)
                for a in range(TAPS):
                    m = [line[p + a] * back[p] for p in range(rows)]
                    while len(m) > 1:
                        m = [m[p] + m[p + 1] for p in range(0, len(m), 2)]
                    total[a * TAPS + b, :, lanes] += m[0]

    lane_blocks(chans, over)

    @pl.when(slot == pl.num_programs(0) - 1)
    def _():
        lines[...] = jnp.zeros_like(lines)
        for i in range(TAPS * TAPS + 2):
            value = total[i] if i < TAPS * TAPS else (gains, scales)[i - TAPS * TAPS][...]
            at = i // share * small.shape[1] + i % share
            lines[at : at + 1, :] = jnp.sum(value, axis=0, keepdims=True)
        for i in range(small.shape[0]):
            small[i] = lines[i * small.shape[1] : (i + 1) * small.shape[1], :].astype(bf16)


def input_kernel(first, count, d_filt, above, below, cotan, kernel, *refs):
    out, pad, wide = refs[-3:]
    slot = pl.program_id(0) + first
    rows, cols, chans = out.shape[2:]

    @pl.when(slot == first)
    def _():
        spread_kernel(wide, kernel)
        clear_padded(pad)

    @pl.when(slot < MOST)
    def _():
        def line_of(r, lanes):
            return d_filt[pl.ds(r * cols, cols), lanes]

        fill_padded(pad, above, line_of, below, rows, cols, chans)
        weight = (slot < count[0]).astype(f32)

        def emit(p, half, lanes, value):
            at = pl.ds(8 * half, 8)
            out[0, 0, p, at, lanes] = value + cotan[0, 0, p, at, lanes].astype(f32) * weight

        stencil(pad, wide, rows, cols, chans, True, emit)

    @pl.when(slot >= MOST)
    def _():
        out[...] = jnp.zeros_like(out)


def body(tiles, cotangent, tile_counts, dw_kernel, ln_gain, fc1_weight, fc2_weight, layer_scale):
    _, slots, rows, cols, chans = tiles.shape
    hidden = fc1_weight.shape[0]
    pixels = rows * cols
    every = MOST * pixels
    gain, scale = ln_gain[None], layer_scale[None]
    above, below = edges(tiles[0, :MOST, :REACH], tiles[0, :MOST, rows - REACH :])

    params = pltpu.CompilerParams(
        vmem_limit_bytes=60 * 1024 * 1024, dimension_semantics=("arbitrary",)
    )
    shape = jax.ShapeDtypeStruct
    brief = pl.CostEstimate(flops=1, bytes_accessed=1, transcendentals=0)
    smem = pl.BlockSpec(memory_space=pltpu.SMEM)
    tile = pl.BlockSpec((1, 1, rows, cols, chans), lambda s: (0, s, 0, 0, 0))
    edge = pl.BlockSpec((1, REACH, cols, chans), lambda s: (s, 0, 0, 0))
    flat = pl.BlockSpec((pixels, chans), lambda s: (s, 0))

    def whole(*dims):
        return pl.BlockSpec(dims, lambda s: (0,) * len(dims))

    pad = pltpu.VMEM((chans // LANES, (rows + 2 * REACH) * PITCH + 8, LANES), f32)
    wide = pltpu.VMEM((TAPS * TAPS, 8, chans), f32)

    chips = SIDE * SIDE
    halves = shape((SIDE, SIDE, SIDE, hidden // (8 * chips), chans), bf16)
    d_edge = shape((MOST, REACH, cols, chans), bf16)
    core = (lax.axis_index("slide") % 2).reshape(1)

    def once(*dims):
        return pl.BlockSpec(dims, lambda s: (0,) * len(dims), pipeline_mode=pl.Buffered(1))

    def block(j):
        return jnp.maximum(j - MOST, 0)

    quarter_of = pl.BlockSpec((SIDE, 1, *halves.shape[2:]), lambda j: (0, block(j), 0, 0, 0))
    live = once(1, MOST, rows, cols, chans)
    mine1, other1, mine2, other2, d_filt, d_head, d_tail, block_out, gain_grad, scale_grad = pl.pallas_call(
        main_kernel,
        grid=(MOST + hidden // BLOCK,),
        in_specs=[
            smem,
            smem,
            once(*above.shape),
            once(*below.shape),
            once(*dw_kernel.shape),
            pl.BlockSpec((BLOCK, chans), lambda j: (block(j), 0)),
            pl.BlockSpec((chans, BLOCK), lambda j: (0, block(j))),
            once(1, chans),
            once(1, chans),
            live,
            live,
        ],
        out_specs=[
            quarter_of,
            quarter_of,
            once(*halves.shape),
            once(*halves.shape),
            once(every, chans),
            once(*d_edge.shape),
            once(*d_edge.shape),
            once(*tiles.shape),
            once(8, chans),
            once(8, chans),
        ],
        out_shape=[
            halves,
            halves,
            halves,
            halves,
            shape((every, chans), f32),
            d_edge,
            d_edge,
            shape(tiles.shape, bf16),
            shape((8, chans), f32),
            shape((8, chans), f32),
        ],
        scratch_shapes=[
            pltpu.VMEM((every, chans), bf16),
            pltpu.VMEM((every, chans), bf16),
            pltpu.VMEM((every, chans), f32),
            pltpu.VMEM((every, LANES), f32),
            pad,
            wide,
            pltpu.VMEM((pixels, chans), f32),
            pltpu.VMEM((chans, every), bf16),
            pltpu.VMEM((chans // LANES, hidden, LANES), f32),
            pltpu.VMEM((BLOCK, chans), f32),
            pltpu.VMEM((every, chans), f32),
            pltpu.VMEM((every, chans), f32),
        ],
        compiler_params=params,
        cost_estimate=brief,
        name="main",
    )(
        core, tile_counts, above, below, dw_kernel, fc1_weight, fc2_weight, gain, scale, tiles, cotangent
    )

    got2, got1 = from_other_core(other2), from_other_core(other1)
    d_above, d_below = edges(d_head, d_tail)

    lines = -(-(TAPS * TAPS + 2) // chips)
    small = shape((chips, -(-lines // 8) * 8, chans), bf16)
    small = pl.pallas_call(
        tap_kernel,
        grid=(MOST,),
        in_specs=[tile, edge, edge, flat, whole(8, chans), whole(8, chans)],
        out_specs=whole(*small.shape),
        out_shape=small,
        scratch_shapes=[pad, wide, pltpu.VMEM((chips * small.shape[1], chans), f32)],
        compiler_params=params,
        cost_estimate=brief,
        name="taps",
    )(tiles, above, below, d_filt, gain_grad, scale_grad)

    small, d_above, d_below, mine1, got1, mine2, got2 = after(
        small, d_above, d_below, mine1, got1, mine2, got2
    )
    share = plane_exchanged(small)[:lines]
    parts2, parts1 = quarters(mine2, got2), quarters(mine1, got1)
    ring2, ring1 = ring_sent(parts2), ring_sent(parts1)
    share, _, _ = after(share, parts2[-1], parts1[-1])
    share, d_filt, d_above, d_below = after(share, d_filt, d_above, d_below)
    small = everywhere(share)

    def input_grads(first, some, earlier, d_filt, d_above, d_below):
        def at(s):
            return jnp.minimum(s + first, MOST - 1)

        tile_at = (1, 1, rows, cols, chans)
        edge_at = pl.BlockSpec((1, REACH, cols, chans), lambda s: (at(s), 0, 0, 0))
        return pl.pallas_call(
            functools.partial(input_kernel, first),
            grid=(some,),
            in_specs=[
                smem,
                pl.BlockSpec((pixels, chans), lambda s: (at(s), 0)),
                edge_at,
                edge_at,
                pl.BlockSpec(tile_at, lambda s: (0, at(s), 0, 0, 0)),
                whole(TAPS, TAPS, chans),
            ]
            + [pl.BlockSpec(memory_space=pl.ANY)] * len(earlier),
            out_specs=pl.BlockSpec(tile_at, lambda s: (0, s + first, 0, 0, 0)),
            out_shape=shape(tiles.shape, f32),
            scratch_shapes=[pad, wide],
            input_output_aliases={6: 0} if earlier else {},
            compiler_params=params,
            cost_estimate=brief,
            name="inputs",
        )(tile_counts, d_filt, d_above, d_below, cotangent, dw_kernel, *earlier)

    grad_input = input_grads(0, 2, [], d_filt, d_above, d_below)

    grad_kernel = small[: TAPS * TAPS].reshape(dw_kernel.shape)
    blocks = jnp.concatenate([total_of(parts2[0], ring2), total_of(parts1[0], ring1)], axis=1)
    blocks, small, grad_input, d_filt = after(blocks, small, grad_input, d_filt)
    grad_input = input_grads(2, slots - 2, [grad_input], d_filt, d_above, d_below)
    sums = plane_exchanged(blocks)
    own = hidden // (8 * chips)
    grad_fc2 = sums[:own].reshape(-1, hidden)
    grad_fc1 = sums[own:]
    return (
        block_out,
        grad_input,
        grad_fc1,
        grad_fc2,
        grad_kernel,
        small[TAPS * TAPS],
        small[TAPS * TAPS + 1],
    )


def solution(mesh):
    in_specs = (
        P("slide", None, "row", None, None),
        P("slide", None, "row", None, None),
        P("slide"),
        P(),
        P(),
        P(),
        P(),
        P(),
    )
    out_specs = (
        P("slide", None, "row", None, None),
        P("slide", None, "row", None, None),
        P(("slide", "row"), None),
        P(("slide", "row"), None),
        P(),
        P(),
        P(),
    )
    return jax.shard_map(body, mesh=mesh, in_specs=in_specs, out_specs=out_specs, check_vma=False)
```
